128 devices in a mesh: section: 8 (over y, x_lo), dp: 16 (over z, x_hi, core).
Axes of the slice: x: 4 (x_hi: 2, x_lo: 2; x = x_hi * 2 + x_lo), y: 4, z: 4, core: 2. Of those that a mesh axis runs over, the one named last changes fastest.
Arguments:
- fwd_input: bfloat16 [8, 2048, 8192], P('section', 'dp'), may hold values from -6 to 6
- bwd_input: bfloat16 [8, 2048, 8192], P('section', 'dp'), may hold values from -6 to 6
- cotangent: bfloat16 [8, 2048, 8192], P('section', 'dp'), may hold values from -6 to 6
- send_buffer: bfloat16 [8, 48, 64, 8192], P('section', 'dp'), may hold values from -6 to 6
- recv_buffer: bfloat16 [8, 48, 64, 8192], P('section', 'dp'), may hold values from -6 to 6
- fwd_ids: int32 [8, 32], P('section', 'dp'), may hold values from 0 to 2
- recv_ids: int32 [8, 32], P('section', 'dp'), may hold values from 0 to 2
- norm_gain: float32 [8, 8192], P('section'), may hold values from 0.1 to 1.9
- w_gate: bfloat16 [8, 8192, 128], P('section'), may hold values from -0.0625 to 0.0625
- w_in: bfloat16 [8, 8192, 128], P('section'), may hold values from -0.0625 to 0.0625
- w_out: bfloat16 [8, 8192, 128], P('section'), may hold values from -0.5 to 0.5
Outputs:
- next_input: bfloat16 [8, 2048, 8192], P('section', 'dp')
- send_rows: bfloat16 [8, 2048, 8192], P('section', 'dp')
- next_cotangent: bfloat16 [8, 2048, 8192], P('section', 'dp')
- weight_grads: float32 [8, 8192, 384], P('section', 'dp')
- gain_grad: float32 [8, 8192], P('section', 'dp')
The draws below stay inside these ranges and needn't reach their ends.
Inputs may be any that keep to these rules, and one draw needn't show every extreme that they name: `fwd_ids`: slot numbers within the replica's own 3 stored samples; repeats may occur. `recv_ids`: slot numbers within the replica's own 3 stored samples; repeats may occur.
All inputs are finite; a program needn't handle non-finite values. Where the reference program divides by a largest or mean magnitude, that divisor is 1e-20 or more.
Results may differ from the reference program's by a relative error of at most 0.019.
Values may be sent and summed in bfloat16 or wider, within the bound.
A program may use at most 192 MiB of HBM per device.

```python
import jax
import jax.numpy as jnp
from jax import lax

D = 8192
R = 128
BLOCK = 128
SEQS = 2
LEN = 64
BUF = 3
SECTIONS = 8
TOKENS = 2048
N_DP = 16


def set_ends(entries, own_key, smallest, top_value):
    index_at = [jax.random.randint(jax.random.fold_in(own_key, axis), (), 0, length) for axis, length in enumerate(entries.shape)]
    main_axis = entries.shape.index(max(entries.shape))
    neighbour = index_at[:main_axis] + [(index_at[main_axis] + 1) % entries.shape[main_axis]] + index_at[main_axis + 1:]
    return entries.at[tuple(index_at)].set(smallest).at[tuple(neighbour)].set(top_value)


def strengthened(result, stream_key, source, target, parts, factor):
    def block_of(dim):
        return (jnp.arange(result.shape[dim]) // (result.shape[dim] // parts)).reshape((-1,) + (1,) * (result.ndim - 1 - dim))

    one_side = jax.random.permutation(stream_key, parts)[block_of(target)]
    second = (block_of(target) + parts // 2) % parts
    return jnp.where((block_of(source) == one_side) | (block_of(source) == second), factor * result, result)


def block_levels(own_key, shape, pieces, least, high):
    def one(position, blocks):
        heights = jax.random.uniform(jax.random.fold_in(jax.random.fold_in(own_key, 6), position), (blocks,), jnp.float32, least / len(pieces), high / len(pieces))
        return jnp.repeat(jnp.exp(heights), shape[position] // blocks).reshape((-1,) + (1,) * (len(shape) - position - 1))

    loudness = one(*pieces[0])
    for cut in pieces[1:]:
        loudness = loudness * one(*cut)
    return loudness


def noise(rng, dims, deviation, reach, shards=(), kind=jnp.bfloat16):
    entries = deviation * jax.random.normal(rng, dims, jnp.float32)
    if shards:
        entries = entries * block_levels(rng, dims, shards, -0.22, 0.18)
    return jnp.clip(entries, -reach, reach).astype(kind)


def noise_with(own_key, shape, scale, limit, pieces, heavy, kind=jnp.bfloat16):
    entries = scale * jax.random.normal(own_key, shape, jnp.float32)
    if pieces:
        entries = entries * block_levels(own_key, shape, pieces, -0.22, 0.18)
    return jnp.clip(strengthened(entries, jax.random.fold_in(own_key, 3), *heavy), -limit, limit).astype(kind)


def setup_inputs(seed: int = 0) -> dict:
    arg_keys = jax.random.split(jax.random.key(seed), 12)
    return {
        "fwd_input": noise(arg_keys[0], (SECTIONS, TOKENS, D), 1.0, 6.0, ((0, 8), (1, 16))),
        "bwd_input": noise_with(arg_keys[1], (SECTIONS, TOKENS, D), 1.0, 6.0, ((0, 8), (1, 16)), (1, 2, 16, 2.0)),
        "cotangent": noise(arg_keys[2], (SECTIONS, TOKENS, D), 1.0, 6.0, ((0, 8), (1, 16))),
        "send_buffer": noise(arg_keys[3], (SECTIONS, BUF * N_DP, LEN, D), 1.0, 6.0, ((0, 8), (1, 16))),
        "recv_buffer": noise(arg_keys[4], (SECTIONS, BUF * N_DP, LEN, D), 1.0, 6.0, ((0, 8), (1, 16))),
        "fwd_ids": set_ends(jax.random.randint(arg_keys[5], (SECTIONS, SEQS * N_DP), 0, BUF), jax.random.fold_in(arg_keys[5], 1), 0, BUF - 1).astype(jnp.int32),
        "recv_ids": set_ends(jax.random.randint(arg_keys[6], (SECTIONS, SEQS * N_DP), 0, BUF), jax.random.fold_in(arg_keys[6], 1), 0, BUF - 1).astype(jnp.int32),
        "norm_gain": jnp.clip(1.0 + 0.18 * jax.random.normal(arg_keys[7], (SECTIONS, D), jnp.float32), 0.1, 1.9),
        "w_gate": noise(arg_keys[8], (SECTIONS, D, R), D ** -0.5, 0.0625, ((0, 8),)),
        "w_in": noise(arg_keys[9], (SECTIONS, D, R), D ** -0.5, 0.0625, ((0, 8),)),
        "w_out": noise(arg_keys[10], (SECTIONS, D, R), R ** -0.5, 0.5, ((0, 8),)),
    }


EPS_NORM = 1e-05
EPS_SCALE = 1e-06

def contract_rows(left, right):
    return lax.dot_general(left, right, (((0,), (0,)), ((), ())), preferred_element_type=jnp.float32)

def contract_cols(left, right):
    return lax.dot_general(left, right, (((1,), (1,)), ((), ())), preferred_element_type=jnp.float32)

def adapter_inner(inputs, gain_row, w_gate, w_in):
    wide = inputs.astype(jnp.float32)
    recip = lax.rsqrt(lax.optimization_barrier(jnp.mean(wide * wide, axis=-1, keepdims=True)) + EPS_NORM)
    normed = (wide * recip * gain_row).astype(jnp.bfloat16)
    gate_pre = jnp.dot(normed, w_gate, preferred_element_type=jnp.float32)
    inner = jnp.dot(normed, w_in, preferred_element_type=jnp.float32)
    sigmoid = jax.nn.sigmoid(gate_pre)
    swish = gate_pre * sigmoid
    mixed = (swish * inner).astype(jnp.bfloat16)
    return (wide, recip, normed, gate_pre, inner, sigmoid, swish, mixed)

def compress(output, stored):
    difference = output - stored.astype(jnp.float32)
    rows = difference.shape[0]
    blocks = difference.reshape(rows, -1, BLOCK)
    block_scale = (lax.optimization_barrier(jnp.max(jnp.abs(blocks), axis=-1)) + EPS_SCALE).astype(jnp.bfloat16)
    quantized = (blocks / block_scale.astype(jnp.float32)[:, :, None]).astype(jnp.bfloat16)
    return (quantized.reshape(rows, -1), block_scale)

def expand(quantized, block_scale):
    rows = quantized.shape[0]
    wide = quantized.astype(jnp.float32).reshape(rows, -1, BLOCK)
    return (wide * block_scale.astype(jnp.float32)[:, :, None]).reshape(rows, -1)

def reference(fwd_input, bwd_input, cotangent, send_buffer, recv_buffer, fwd_ids, recv_ids, norm_gain, w_gate, w_in, w_out):
    owner = jnp.arange(SEQS * N_DP, dtype=jnp.int32) // SEQS * BUF

    def pick(buffer, slot_ids):
        slots = slot_ids.astype(jnp.int32) + owner
        return jnp.take(buffer, slots, axis=0).reshape(TOKENS, D)

    def forward_section(packed):
        inputs, buffer, slot_ids, gain_row, gate_w, in_w, out_w = packed
        saved = adapter_inner(inputs, gain_row, gate_w, in_w)
        output = saved[0] + contract_cols(saved[7], out_w)
        stored = pick(buffer, slot_ids)
        quantized, block_scale = compress(output, stored)
        rows_new = (stored.astype(jnp.float32) + expand(quantized, block_scale)).astype(jnp.bfloat16)
        return (quantized, block_scale, rows_new)
    quantized, block_scale, send_rows = lax.map(forward_section, (fwd_input, send_buffer, fwd_ids, norm_gain, w_gate, w_in, w_out))
    arrived_q = jnp.concatenate([jnp.zeros_like(quantized[:1]), quantized[:-1]], axis=0)
    arrived_s = jnp.concatenate([jnp.zeros_like(block_scale[:1]), block_scale[:-1]], axis=0)

    def receive_section(packed):
        buffer, slot_ids, quant_part, scale_part = packed
        arrived = pick(buffer, slot_ids).astype(jnp.float32)
        return (arrived + expand(quant_part, scale_part)).astype(jnp.bfloat16)
    next_input = lax.map(receive_section, (recv_buffer, recv_ids, arrived_q, arrived_s))

    def backward_section(packed):
        inputs, upstream_in, gain_row, gate_w, in_w, out_w = packed
        wide, recip, normed, gate_pre, inner, sigmoid, swish, mixed = adapter_inner(inputs, gain_row, gate_w, in_w)
        grad_mixed = jnp.dot(upstream_in, out_w, preferred_element_type=jnp.float32)
        grad_gate = (grad_mixed * inner * sigmoid * (1.0 + gate_pre * (1.0 - sigmoid))).astype(jnp.bfloat16)
        grad_inner = (grad_mixed * swish).astype(jnp.bfloat16)
        terms = jnp.concatenate([contract_rows(normed, grad_gate), contract_rows(normed, grad_inner), contract_rows(upstream_in, mixed)], axis=1)
        grad_normed = contract_cols(grad_gate, gate_w) + contract_cols(grad_inner, in_w)
        gain_term = lax.optimization_barrier(jnp.sum(grad_normed * wide * recip, axis=0))
        scaled = grad_normed * gain_row
        grad_inputs = recip * scaled - wide * recip * recip * recip * lax.optimization_barrier(jnp.mean(wide * scaled, axis=-1, keepdims=True))
        passed = (upstream_in.astype(jnp.float32) + grad_inputs).astype(jnp.bfloat16)
        return (passed, terms, gain_term)
    passed, weight_grads, gain_grad = lax.map(backward_section, (bwd_input, cotangent, norm_gain, w_gate, w_in, w_out))
    next_cotangent = jnp.concatenate([passed[1:], jnp.zeros_like(passed[:1])], axis=0)
    return (next_input, send_rows, next_cotangent, weight_grads, gain_grad)
```

```python
import functools

import jax
import jax.numpy as jnp
from jax import lax
from jax.experimental import pallas as pl
from jax.experimental.pallas import tpu as pltpu
from jax.sharding import PartitionSpec as P

MESH = pl.DeviceIdType.MESH
F32 = jnp.float32
BF16 = jnp.bfloat16

BLOCK = 128
EPS_NORM = 1e-05
EPS_SCALE = 1e-06

TOK = 128
HALF = 64
D = 8192
R = 128
CW = 512
NC = D // CW
PIECES = 4
PW = D // PIECES
SECTIONS = 8


def dot_nn(a, b):
    return jnp.dot(a, b, preferred_element_type=F32)


def dot_nt(a, b):
    return lax.dot_general(a, b, (((1,), (1,)), ((), ())), preferred_element_type=F32)


def at(i):
    return pl.ds(pl.multiple_of(i * CW, CW), CW)


def kernel(
    ids_f, ids_r, fin, bin_, cot, sbuf, rbuf, gain, wg, wi, wo,
    next_input, send_rows, next_cot, wgrad, ggrad,
    fin_v, bin_v, cot_v, sb_v, rb_v, gain_v, w_v, wo_v,
    acc, acc2, ss, gm, mx, gcat, grad_t, mixed_t, krow,
    fs, fr, bs, ni, sr, zero,
    part, core_in, chip, z_in, x_out, x_in, wg_v, gg_v,
    load_a, load_b, load_c, fs_s, fs_r, bs_s, bs_r, out_s, core_s, core_r, z_s, z_r, x_sem,
):
    s = lax.axis_index("section")
    d = lax.axis_index("dp")
    core = lax.rem(d, 2)
    xh = lax.rem(d // 2, 2)
    z = d // 4
    has_next = s < SECTIONS - 1
    has_prev = s > 0

    def load_piece(p):
        cols = pl.ds(p * PW, PW)
        return (
            pltpu.make_async_copy(fin.at[:, cols], fin_v.at[:, cols], load_a.at[p, 0]),
            pltpu.make_async_copy(wg.at[cols], w_v.at[cols, pl.ds(0, R)], load_a.at[p, 1]),
            pltpu.make_async_copy(wi.at[cols], w_v.at[cols, pl.ds(R, R)], load_a.at[p, 2]),
        )

    gain_load = pltpu.make_async_copy(gain, gain_v, load_b.at[0])
    wo_load = pltpu.make_async_copy(wo, wo_v, load_b.at[1])
    sb_load = pltpu.make_async_copy(sbuf, sb_v, load_b.at[2])
    bin_load = pltpu.make_async_copy(bin_, bin_v, load_b.at[3])
    cot_load = pltpu.make_async_copy(cot, cot_v, load_b.at[4])
    rb_load = pltpu.make_async_copy(rbuf, rb_v, load_b.at[5])
    gain_load.start()
    for p in range(PIECES):
        for c in load_piece(p):
            c.start()
    for c in (wo_load, sb_load, bin_load, cot_load, rb_load):
        c.start()

    bar = pltpu.get_barrier_semaphore()

    def greet(to):
        pl.semaphore_signal(bar, inc=1, device_id=to, device_id_type=MESH)

    sibling = (s, d + 1 - 2 * core)
    across = (s, d + 2 - 4 * xh)

    def z_peer(step):
        return (s, lax.rem(z + step, 4) * 4 + xh * 2 + core)

    greet(sibling)
    greet(across)
    for step in (1, 2, 3):
        greet(z_peer(step))

    greet((lax.rem(s + 1, SECTIONS), d))
    greet((lax.rem(s + SECTIONS - 1, SECTIONS), d))

    acc[...] = jnp.zeros_like(acc)
    ss[...] = jnp.zeros_like(ss)
    gain_load.wait()

    def norm_step(x_ref, c):
        cols = at(c)
        x = x_ref[:, cols].astype(F32)
        xg = (x * gain_v[:, cols]).astype(BF16)
        sq = x * x
        total = sq[:, 0:BLOCK]
        for b in range(1, CW // BLOCK):
            total += sq[:, b * BLOCK : (b + 1) * BLOCK]
        return total, dot_nn(xg, w_v[cols, :])

    for p in range(PIECES):
        for c in load_piece(p):
            c.wait()

        def f1(c, _):
            sq, prod = norm_step(fin_v, c)
            ss[...] += sq
            acc[...] += prod
            return 0

        lax.fori_loop(p * (NC // PIECES), (p + 1) * (NC // PIECES), f1, 0)

    recip = lax.rsqrt(jnp.sum(ss[...], axis=-1, keepdims=True) / D + EPS_NORM)
    gate_pre = acc[:, 0:R] * recip
    inner = acc[:, R : 2 * R] * recip
    mx[...] = (gate_pre * jax.nn.sigmoid(gate_pre) * inner).astype(BF16)

    pl.semaphore_wait(bar, 7)

    wo_load.wait()
    sb_load.wait()

    def fwd_copy(c):
        return pltpu.make_async_remote_copy(
            src_ref=fs.at[c], dst_ref=fr.at[c], send_sem=fs_s.at[c], recv_sem=fs_r.at[c],
            device_id=(s + 1, d), device_id_type=MESH,
        )

    def rows_out(c):
        return pltpu.make_async_copy(sr.at[:, at(c)], send_rows.at[:, at(c)], out_s.at[0, c])

    def f2(c, _):
        cols = at(c)
        update = dot_nt(mx[...], wo_v[cols, :])
        for h in range(2):
            rows = slice(h * HALF, (h + 1) * HALF)
            slot = ids_f[0, h]
            stored = sb_v[slot, :, cols].astype(F32)
            diff = fin_v[rows, cols].astype(F32) + update[rows] - stored
            for b in range(CW // BLOCK):
                lanes = slice(b * BLOCK, (b + 1) * BLOCK)
                part_diff = diff[:, lanes]
                top = jnp.max(jnp.abs(part_diff), axis=-1, keepdims=True)
                scale = (top + EPS_SCALE).astype(BF16).astype(F32)
                quantized = (part_diff / scale).astype(BF16)
                product = scale * quantized.astype(F32)
                fs[c, rows, lanes] = product.astype(BF16)
                lane_at = pl.ds(pl.multiple_of(c * CW + b * BLOCK, BLOCK), BLOCK)
                sr[rows, lane_at] = (stored[:, lanes] + product).astype(BF16)

        @pl.when(has_next)
        def _():
            fwd_copy(c).start()

        rows_out(c).start()
        return 0

    lax.fori_loop(0, NC, f2, 0)

    acc2[...] = jnp.zeros_like(acc2)
    ss[...] = jnp.zeros_like(ss)
    gm[...] = jnp.zeros_like(gm)
    bin_load.wait()
    cot_load.wait()

    def b1(c, _):
        sq, prod = norm_step(bin_v, c)
        ss[...] += sq
        acc2[...] += prod
        gm[...] += dot_nn(cot_v[:, at(c)], wo_v[at(c), :])
        return 0

    lax.fori_loop(0, NC, b1, 0)
    recip_b = lax.rsqrt(jnp.sum(ss[...], axis=-1, keepdims=True) / D + EPS_NORM)
    gate_b = acc2[:, 0:R] * recip_b
    inner_b = acc2[:, R : 2 * R] * recip_b
    sig = jax.nn.sigmoid(gate_b)
    swish = gate_b * sig
    grad_mixed = gm[...]
    gg = grad_mixed * inner_b * sig * (1.0 + gate_b * (1.0 - sig)) * recip_b
    gi = grad_mixed * swish * recip_b
    gcat[:, 0:R] = gg.astype(BF16)
    gcat[:, R : 2 * R] = gi.astype(BF16)
    grad_t[0:R, :] = gg.T.astype(BF16)
    grad_t[R : 2 * R, :] = gi.T.astype(BF16)
    mixed_t[...] = (swish * inner_b).T.astype(BF16)
    dots = jnp.sum(gg * gate_b + gi * inner_b, axis=-1, keepdims=True)
    krow[...] = jnp.broadcast_to(dots * recip_b * (1.0 / D), (TOK, BLOCK))

    def core_copy(i):
        return pltpu.make_async_remote_copy(
            src_ref=part.at[2 * i + 1 - core], dst_ref=core_in.at[i],
            send_sem=core_s.at[i], recv_sem=core_r.at[i],
            device_id=sibling, device_id_type=MESH,
        )

    def b3(j, _):
        cols = at(j)
        part[j, 0 : 2 * R, :] = dot_nn(grad_t[...], bin_v[:, cols]).astype(BF16)
        part[j, 2 * R : 3 * R, :] = dot_nn(mixed_t[...], cot_v[:, cols]).astype(BF16)

        @pl.when(lax.rem(j, 2) != core)
        def _():
            core_copy(j // 2).start()

        return 0

    lax.fori_loop(0, NC, b3, 0)

    def bwd_copy(c):
        return pltpu.make_async_remote_copy(
            src_ref=bs.at[c], dst_ref=next_cot.at[:, at(c)], send_sem=bs_s.at[c], recv_sem=bs_r.at[c],
            device_id=(s - 1, d), device_id_type=MESH,
        )

    def zero_out(c):
        return pltpu.make_async_copy(zero, next_cot.at[:, at(c)], out_s.at[1, c])

    zero[...] = jnp.zeros_like(zero)

    def b2(c, _):
        cols = at(c)
        grad_normed = dot_nt(gcat[...], w_v[cols, :])
        x = bin_v[:, cols].astype(F32)
        for b in range(CW // BLOCK):
            lanes = slice(b * BLOCK, (b + 1) * BLOCK)
            lane_at = pl.ds(pl.multiple_of(c * CW + b * BLOCK, BLOCK), BLOCK)
            passed = (
                cot_v[:, lane_at].astype(F32)
                + grad_normed[:, lanes] * gain_v[:, lane_at]
                - x[:, lanes] * krow[...]
            )
            bs[c, :, lanes] = passed.astype(BF16)

        @pl.when(has_prev)
        def _():
            bwd_copy(c).start()

        @pl.when(jnp.logical_not(has_next))
        def _():
            zero_out(c).start()

        return 0

    lax.fori_loop(0, NC, b2, 0)

    def z_copy(step, h, i):
        return pltpu.make_async_remote_copy(
            src_ref=chip.at[i], dst_ref=z_in.at[step - 1, h],
            send_sem=z_s.at[step - 1, h], recv_sem=z_r.at[step - 1, h],
            device_id=z_peer(step), device_id_type=MESH,
        )

    def chip_sum(k, _):
        h = jnp.where(k < 4, 1 - xh, xh)
        step = lax.rem(k + 1, 4)
        i = lax.rem(z + step, 4) * 2 + h
        core_copy(i).wait_recv()

        def rows_sum(t, _):
            rows = pl.ds(pl.multiple_of(t * 64, 64), 64)
            chip[i, rows, :] = (
                part[2 * i + core, rows, :].astype(F32) + core_in[i, rows, :].astype(F32)
            ).astype(BF16)
            return 0

        lax.fori_loop(0, 6, rows_sum, 0)

        @pl.when(step > 0)
        def _():
            z_copy(step, h, i).start()

        return 0

    lax.fori_loop(0, 8, chip_sum, 0)

    rb_load.wait()

    def input_out(c):
        return pltpu.make_async_copy(ni.at[:, at(c)], next_input.at[:, at(c)], out_s.at[2, c])

    def receive(c, _):
        @pl.when(has_prev)
        def _():
            fwd_copy(c).wait_recv()

        @pl.when(jnp.logical_not(has_prev))
        def _():
            fr[c] = jnp.zeros((TOK, CW), BF16)

        cols = at(c)
        for h in range(2):
            rows = slice(h * HALF, (h + 1) * HALF)
            arrived = rb_v[ids_r[0, h], :, cols].astype(F32)
            ni[rows, cols] = (arrived + fr[c, rows, :].astype(F32)).astype(BF16)
        input_out(c).start()
        return 0

    lax.fori_loop(0, NC, receive, 0)

    x_copy = pltpu.make_async_remote_copy(
        src_ref=x_out, dst_ref=x_in, send_sem=x_sem.at[0], recv_sem=x_sem.at[1],
        device_id=across, device_id_type=MESH,
    )

    def z_sum(h, rows):
        total = chip[2 * z + h, rows, :].astype(F32)
        for step in range(3):
            total += z_in[step, h, rows, :].astype(F32)
        return total

    for step in (1, 2, 3):
        z_copy(step, 1 - xh, 0).wait_recv()

    def other_sum(t, _):
        rows = pl.ds(pl.multiple_of(t * 64, 64), 64)
        x_out[rows, :] = z_sum(1 - xh, rows).astype(BF16)
        return 0

    lax.fori_loop(0, 6, other_sum, 0)
    x_copy.start()
    for step in (1, 2, 3):
        z_copy(step, xh, 0).wait_recv()
    x_copy.wait_recv()

    def final(t, _):
        lanes = pl.ds(pl.multiple_of(t * BLOCK, BLOCK), BLOCK)
        mine = pl.ds(pl.multiple_of(d * CW + t * BLOCK, BLOCK), BLOCK)
        gain_row = gain_v[:, mine]
        weighted = jnp.zeros((BLOCK, R), F32)
        for a in range(3):
            rows = slice(a * R, (a + 1) * R)
            total = chip[2 * z + xh, rows, lanes].astype(F32)
            for step in range(3):
                total += z_in[step, xh, rows, lanes].astype(F32)
            total += x_in[rows, lanes].astype(F32)
            if a < 2:
                w_rows = w_v[mine, a * R : (a + 1) * R].astype(F32)
                weighted += w_rows * total.T
                total = total * gain_row
            wg_v[lanes, a * R : (a + 1) * R] = total.T
        gg_v[:, lanes] = jnp.sum(weighted.T, axis=0, keepdims=True)
        return 0

    lax.fori_loop(0, CW // BLOCK, final, 0)
    wgrad_out = pltpu.make_async_copy(wg_v, wgrad, load_c.at[0])
    ggrad_out = pltpu.make_async_copy(gg_v, ggrad, load_c.at[1])
    wgrad_out.start()
    ggrad_out.start()

    x_copy.wait_send()

    def drain(c, _):
        @pl.when(has_next)
        def _():
            fwd_copy(c).wait_send()
            bwd_copy(c).wait_recv()

        @pl.when(has_prev)
        def _():
            bwd_copy(c).wait_send()

        @pl.when(jnp.logical_not(has_next))
        def _():
            zero_out(c).wait()

        rows_out(c).wait()
        input_out(c).wait()
        return 0

    lax.fori_loop(0, NC, drain, 0)

    def drain_core(i, _):
        core_copy(i).wait_send()
        return 0

    lax.fori_loop(0, 8, drain_core, 0)
    for step in (1, 2, 3):
        for h in range(2):
            z_copy(step, h, 0).wait_send()
    wgrad_out.wait()
    ggrad_out.wait()


def local(
    fwd_input, bwd_input, cotangent, send_buffer, recv_buffer,
    fwd_ids, recv_ids, norm_gain, w_gate, w_in, w_out,
):
    any_spec = pl.BlockSpec(memory_space=pl.ANY)
    smem = pl.BlockSpec(memory_space=pltpu.SMEM)
    dma = pltpu.SemaphoreType.DMA
    wide = (TOK, D)
    chunks = (NC, TOK, CW)
    block = (3 * R, CW)
    outs = pl.pallas_call(
        kernel,
        out_shape=[
            jax.ShapeDtypeStruct(wide, BF16),
            jax.ShapeDtypeStruct(wide, BF16),
            jax.ShapeDtypeStruct(wide, BF16),
            jax.ShapeDtypeStruct((CW, 3 * R), F32),
            jax.ShapeDtypeStruct((1, CW), F32),
        ],
        in_specs=[smem, smem] + [any_spec] * 9,
        out_specs=[any_spec] * 5,
        scratch_shapes=[
            pltpu.VMEM(wide, BF16),
            pltpu.VMEM(wide, BF16),
            pltpu.VMEM(wide, BF16),
            pltpu.VMEM((3, HALF, D), BF16),
            pltpu.VMEM((3, HALF, D), BF16),
            pltpu.VMEM((1, D), F32),
            pltpu.VMEM((D, 2 * R), BF16),
            pltpu.VMEM((D, R), BF16),
            pltpu.VMEM((TOK, 2 * R), F32),
            pltpu.VMEM((TOK, 2 * R), F32),
            pltpu.VMEM((TOK, BLOCK), F32),
            pltpu.VMEM((TOK, R), F32),
            pltpu.VMEM((TOK, R), BF16),
            pltpu.VMEM((TOK, 2 * R), BF16),
            pltpu.VMEM((2 * R, TOK), BF16),
            pltpu.VMEM((R, TOK), BF16),
            pltpu.VMEM((TOK, BLOCK), F32),
            pltpu.VMEM(chunks, BF16),
            pltpu.VMEM(chunks, BF16),
            pltpu.VMEM(chunks, BF16),
            pltpu.VMEM(wide, BF16),
            pltpu.VMEM(wide, BF16),
            pltpu.VMEM((TOK, CW), BF16),
            pltpu.VMEM((NC,) + block, BF16),
            pltpu.VMEM((8,) + block, BF16),
            pltpu.VMEM((8,) + block, BF16),
            pltpu.VMEM((3, 2) + block, BF16),
            pltpu.VMEM(block, BF16),
            pltpu.VMEM(block, BF16),
            pltpu.VMEM((CW, 3 * R), F32),
            pltpu.VMEM((1, CW), F32),
            dma((PIECES, 3)),
            dma((6,)),
            dma((2,)),
            dma((NC,)),
            dma((NC,)),
            dma((NC,)),
            dma((NC,)),
            dma((3, NC)),
            dma((8,)),
            dma((8,)),
            dma((3, 2)),
            dma((3, 2)),
            dma((2,)),
        ],
        compiler_params=pltpu.CompilerParams(
            collective_id=0, has_side_effects=True, vmem_limit_bytes=58 << 20
        ),
        cost_estimate=pl.CostEstimate(
            flops=2 * 11 * TOK * D * R, bytes_accessed=28 << 20, transcendentals=4 * TOK * R
        ),
    )(
        fwd_ids, recv_ids, fwd_input[0], bwd_input[0], cotangent[0], send_buffer[0],
        recv_buffer[0], norm_gain, w_gate[0], w_in[0], w_out[0],
    )
    return (outs[0][None], outs[1][None], outs[2][None], outs[3][None], outs[4])


def solution(mesh):
    return jax.shard_map(
        local,
        mesh=mesh,
        in_specs=(
            P("section", "dp", None),
            P("section", "dp", None),
            P("section", "dp", None),
            P("section", "dp", None, None),
            P("section", "dp", None, None),
            P("section", "dp"),
            P("section", "dp"),
            P("section", None),
            P("section", None, None),
            P("section", None, None),
            P("section", None, None),
        ),
        out_specs=(
            P("section", "dp", None),
            P("section", "dp", None),
            P("section", "dp", None),
            P("section", "dp", None),
            P("section", "dp"),
        ),
        check_vma=False,
    )
```

```python
import functools

import jax
import jax.numpy as jnp
from jax import lax
from jax.experimental import pallas as pl
from jax.experimental.pallas import tpu as pltpu
from jax.sharding import PartitionSpec as P

MESH = pl.DeviceIdType.MESH
F32 = jnp.float32
BF16 = jnp.bfloat16

BLOCK = 128
EPS_NORM = 1e-05
EPS_SCALE = 1e-06

TOK = 128
HALF = 64
D = 8192
R = 128
CW = 512
NC = D // CW
PIECES = 4
PW = D // PIECES
FIN, BIN, COT, WG, WI, WO = range(6)
RELAYS = 12
SECTIONS = 8
PEERS = 9
LATE = 13


def dot_nn(a, b):
    return jnp.dot(a, b, preferred_element_type=F32)


def dot_nt(a, b):
    return lax.dot_general(a, b, (((1,), (1,)), ((), ())), preferred_element_type=F32)


def at(i):
    return pl.ds(pl.multiple_of(i * CW, CW), CW)


def kernel(
    ids_f, ids_r, fin, bin_, cot, sbuf, rbuf, gain, wg, wi, wo,
    next_input, send_rows, next_cot, wgrad, ggrad,
    fin_v, bin_v, cot_v, sb_v, rb_v, gain_v, w_v, wo_v,
    acc, acc2, ss, gm, mx, gcat, grad_t, mixed_t, krow,
    fs, fr, bs, relay,
    part, core_in, chip, z_in, x_out, x_in,
    load_a, load_b, fs_s, fs_r, bs_s, bs_r, rl_s, rl_r, core_s, core_r, z_s, z_r, x_sem,
):
    s = lax.axis_index("section")
    d = lax.axis_index("dp")
    core = lax.rem(d, 2)
    xh = lax.rem(d // 2, 2)
    z = d // 4
    has_next = s < SECTIONS - 1
    has_prev = s > 0

    even = lax.rem(s, 2) == 0

    def piece(kind, p):
        cols = pl.ds(p * PW, PW)
        sem = load_a.at[kind, p]
        if kind == FIN:
            return pltpu.make_async_copy(fin.at[:, cols], fin_v.at[:, cols], sem)
        if kind == BIN:
            return pltpu.make_async_copy(bin_.at[:, cols], bin_v.at[:, cols], sem)
        if kind == COT:
            return pltpu.make_async_copy(cot.at[:, cols], cot_v.at[:, cols], sem)
        if kind == WG:
            return pltpu.make_async_copy(wg.at[cols], w_v.at[cols, pl.ds(0, R)], sem)
        if kind == WI:
            return pltpu.make_async_copy(wi.at[cols], w_v.at[cols, pl.ds(R, R)], sem)
        return pltpu.make_async_copy(wo.at[cols], wo_v.at[cols], sem)

    def start_pieces(*kinds):
        for p in range(PIECES):
            for kind in kinds:
                piece(kind, p).start()

    gain_load = pltpu.make_async_copy(gain, gain_v, load_b.at[0])
    sb_load = pltpu.make_async_copy(sbuf, sb_v, load_b.at[1])
    rb_load = pltpu.make_async_copy(rbuf, rb_v, load_b.at[2])
    gain_load.start()

    @pl.when(even)
    def _():
        start_pieces(FIN, WG, WI)
        start_pieces(WO)
        sb_load.start()

    @pl.when(jnp.logical_not(even))
    def _():
        start_pieces(BIN, WG, WI, COT, WO)

    bar = pltpu.get_barrier_semaphore()

    def greet(to):
        pl.semaphore_signal(bar, inc=1, device_id=to, device_id_type=MESH)

    sibling = (s, d + 1 - 2 * core)
    across = (s, d + 2 - 4 * xh)

    def z_peer(step):
        return (s, lax.rem(z + step, 4) * 4 + xh * 2 + core)

    greet(sibling)
    greet(across)
    for step in (1, 2, 3):
        greet(z_peer(step))

    for step in (1, 2, SECTIONS - 2, SECTIONS - 1):
        greet((lax.rem(s + step, SECTIONS), d))

    gain_load.wait()

    def norm_step(x_ref, c):
        cols = at(c)
        x = x_ref[:, cols].astype(F32)
        xg = (x * gain_v[:, cols]).astype(BF16)
        sq = x * x
        total = sq[:, 0:BLOCK]
        for b in range(1, CW // BLOCK):
            total += sq[:, b * BLOCK : (b + 1) * BLOCK]
        return total, dot_nn(xg, w_v[cols, :])

    fwd_via = jnp.where(jnp.logical_and(jnp.logical_not(even), has_next), 2 * (s + 1), 0)
    bwd_via = jnp.where(jnp.logical_and(even, has_prev), 16 - 2 * s, 0)
    fwd_relays = jnp.where(jnp.logical_not(even), 2 * (s - 1), 0)
    bwd_relays = jnp.where(jnp.logical_and(even, s <= 4), 12 - 2 * s, 0)

    def remote(src, dst, send, recv, to):
        return pltpu.make_async_remote_copy(
            src_ref=src, dst_ref=dst, send_sem=send, recv_sem=recv,
            device_id=(to, d), device_id_type=MESH,
        )

    def fwd_copy(c):
        return remote(fs.at[c], fr.at[c], fs_s.at[c], fs_r.at[c], s + 1)

    def fwd_detour(c):
        return remote(fs.at[c], relay.at[c], fs_s.at[c], rl_r.at[c], s + 2)

    def fwd_onward(c):
        return remote(relay.at[c], fr.at[c], rl_s.at[c], fs_r.at[c], s - 1)

    def bwd_copy(c):
        return remote(bs.at[c], next_cot.at[:, at(c)], bs_s.at[c], bs_r.at[c], s - 1)

    def bwd_detour(c):
        return remote(bs.at[c], relay.at[c], bs_s.at[c], rl_r.at[c], s - 2)

    def bwd_onward(c):
        return remote(relay.at[c], next_cot.at[:, at(c)], rl_s.at[c], bs_r.at[c], s + 1)

    def core_copy(i):
        return pltpu.make_async_remote_copy(
            src_ref=part.at[2 * i + 1 - core], dst_ref=core_in.at[i],
            send_sem=core_s.at[i], recv_sem=core_r.at[i],
            device_id=sibling, device_id_type=MESH,
        )

    def forward(first):
        acc[...] = jnp.zeros_like(acc)
        ss[...] = jnp.zeros_like(ss)

        def f1(c, _):
            sq, prod = norm_step(fin_v, c)
            ss[...] += sq
            acc[...] += prod
            return 0

        for p in range(PIECES):
            piece(FIN, p).wait()

            @pl.when(first)
            def _():
                piece(WG, p).wait()
                piece(WI, p).wait()

            lax.fori_loop(p * (NC // PIECES), (p + 1) * (NC // PIECES), f1, 0)

        @pl.when(first)
        def _():
            start_pieces(BIN, COT)
            rb_load.start()

        recip = lax.rsqrt(jnp.sum(ss[...], axis=-1, keepdims=True) / D + EPS_NORM)
        gate_pre = acc[:, 0:R] * recip
        inner = acc[:, R : 2 * R] * recip
        mx[...] = (gate_pre * jax.nn.sigmoid(gate_pre) * inner).astype(BF16)

        @pl.when(first)
        def _():
            for p in range(PIECES):
                piece(WO, p).wait()
            pl.semaphore_wait(bar, PEERS)

        sb_load.wait()

        def f2(c, _):
            cols = at(c)
            update = dot_nt(mx[...], wo_v[cols, :])
            for h in range(2):
                rows = slice(h * HALF, (h + 1) * HALF)
                slot = ids_f[0, h]
                stored = sb_v[slot, :, cols].astype(F32)
                diff = fin_v[rows, cols].astype(F32) + update[rows] - stored
                for b in range(CW // BLOCK):
                    lanes = slice(b * BLOCK, (b + 1) * BLOCK)
                    part_diff = diff[:, lanes]
                    top = jnp.max(jnp.abs(part_diff), axis=-1, keepdims=True)
                    scale = (top + EPS_SCALE).astype(BF16).astype(F32)
                    quantized = (part_diff / scale).astype(BF16)
                    product = scale * quantized.astype(F32)
                    fs[c, rows, lanes] = product.astype(BF16)
                    lane_at = pl.ds(pl.multiple_of(c * CW + b * BLOCK, BLOCK), BLOCK)
                    send_rows[rows, lane_at] = (stored[:, lanes] + product).astype(BF16)

            @pl.when(jnp.logical_and(has_next, c >= fwd_via))
            def _():
                fwd_copy(c).start()

            @pl.when(c < fwd_via)
            def _():
                fwd_detour(c).start()

            return 0

        lax.fori_loop(0, NC, f2, 0)

    def backward(first):
        acc2[...] = jnp.zeros_like(acc2)
        ss[...] = jnp.zeros_like(ss)
        gm[...] = jnp.zeros_like(gm)

        def b1(c, _):
            sq, prod = norm_step(bin_v, c)
            ss[...] += sq
            acc2[...] += prod
            gm[...] += dot_nn(cot_v[:, at(c)], wo_v[at(c), :])
            return 0

        for p in range(PIECES):
            piece(BIN, p).wait()
            piece(COT, p).wait()

            @pl.when(first)
            def _():
                for kind in (WG, WI, WO):
                    piece(kind, p).wait()

            lax.fori_loop(p * (NC // PIECES), (p + 1) * (NC // PIECES), b1, 0)

        @pl.when(first)
        def _():
            start_pieces(FIN)
            sb_load.start()
            rb_load.start()

        recip_b = lax.rsqrt(jnp.sum(ss[...], axis=-1, keepdims=True) / D + EPS_NORM)
        gate_b = acc2[:, 0:R] * recip_b
        inner_b = acc2[:, R : 2 * R] * recip_b
        sig = jax.nn.sigmoid(gate_b)
        swish = gate_b * sig
        grad_mixed = gm[...]
        gg = grad_mixed * inner_b * sig * (1.0 + gate_b * (1.0 - sig)) * recip_b
        gi = grad_mixed * swish * recip_b
        gcat[:, 0:R] = gg.astype(BF16)
        gcat[:, R : 2 * R] = gi.astype(BF16)
        grad_t[0:R, :] = gg.T.astype(BF16)
        grad_t[R : 2 * R, :] = gi.T.astype(BF16)
        mixed_t[...] = (swish * inner_b).T.astype(BF16)
        dots = jnp.sum(gg * gate_b + gi * inner_b, axis=-1, keepdims=True)
        krow[...] = jnp.broadcast_to(dots * recip_b * (1.0 / D), (TOK, BLOCK))

        @pl.when(first)
        def _():
            pl.semaphore_wait(bar, PEERS)

        def b2(c, _):
            cols = at(c)
            grad_normed = dot_nt(gcat[...], w_v[cols, :])
            x = bin_v[:, cols].astype(F32)
            for b in range(CW // BLOCK):
                lanes = slice(b * BLOCK, (b + 1) * BLOCK)
                lane_at = pl.ds(pl.multiple_of(c * CW + b * BLOCK, BLOCK), BLOCK)
                passed = (
                    cot_v[:, lane_at].astype(F32)
                    + grad_normed[:, lanes] * gain_v[:, lane_at]
                    - x[:, lanes] * krow[...]
                )
                bs[c, :, lanes] = passed.astype(BF16)

            @pl.when(jnp.logical_and(has_prev, c >= bwd_via))
            def _():
                bwd_copy(c).start()

            @pl.when(c < bwd_via)
            def _():
                bwd_detour(c).start()

            @pl.when(jnp.logical_not(has_next))
            def _():
                next_cot[:, cols] = jnp.zeros((TOK, CW), BF16)

            return 0

        lax.fori_loop(0, NC, b2, 0)

        def b3(j, _):
            cols = at(j)
            part[j, 0 : 2 * R, :] = dot_nn(grad_t[...], bin_v[:, cols]).astype(BF16)
            part[j, 2 * R : 3 * R, :] = dot_nn(mixed_t[...], cot_v[:, cols]).astype(BF16)

            @pl.when(lax.rem(j, 2) != core)
            def _():
                core_copy(j // 2).start()

            return 0

        lax.fori_loop(0, NC, b3, 0)

    def half(turn, _):
        @pl.when(lax.rem(s + turn, 2) == 0)
        def _():
            forward(turn == 0)

        @pl.when(lax.rem(s + turn, 2) == 1)
        def _():
            backward(turn == 0)

        return 0

    lax.fori_loop(0, 2, half, 0)

    def z_copy(step, h, i):
        return pltpu.make_async_remote_copy(
            src_ref=chip.at[i], dst_ref=z_in.at[step - 1, h],
            send_sem=z_s.at[step - 1, h], recv_sem=z_r.at[step - 1, h],
            device_id=z_peer(step), device_id_type=MESH,
        )

    def chip_sum(k, _):
        h = jnp.where(k < 4, 1 - xh, xh)
        step = lax.rem(k + 1, 4)
        i = lax.rem(z + step, 4) * 2 + h
        core_copy(i).wait_recv()

        def rows_sum(t, _):
            rows = pl.ds(pl.multiple_of(t * 64, 64), 64)
            chip[i, rows, :] = (
                part[2 * i + core, rows, :].astype(F32) + core_in[i, rows, :].astype(F32)
            ).astype(BF16)
            return 0

        lax.fori_loop(0, 6, rows_sum, 0)

        @pl.when(step > 0)
        def _():
            z_copy(step, h, i).start()

        return 0

    lax.fori_loop(0, 8, chip_sum, 0)

    def hand_on(c, _):
        @pl.when(even)
        def _():
            bwd_detour(c).wait_recv()
            bwd_onward(c).start()

        @pl.when(jnp.logical_not(even))
        def _():
            fwd_detour(c).wait_recv()
            fwd_onward(c).start()

        return 0

    lax.fori_loop(0, fwd_relays + bwd_relays, hand_on, 0)

    x_copy = pltpu.make_async_remote_copy(
        src_ref=x_out, dst_ref=x_in, send_sem=x_sem.at[0], recv_sem=x_sem.at[1],
        device_id=across, device_id_type=MESH,
    )

    def z_sum(h, rows):
        total = chip[2 * z + h, rows, :].astype(F32)
        for step in range(3):
            total += z_in[step, h, rows, :].astype(F32)
        return total

    for step in (1, 2, 3):
        z_copy(step, 1 - xh, 0).wait_recv()

    def other_sum(t, _):
        rows = pl.ds(pl.multiple_of(t * 64, 64), 64)
        x_out[rows, :] = z_sum(1 - xh, rows).astype(BF16)
        return 0

    lax.fori_loop(0, 6, other_sum, 0)
    x_copy.start()

    rb_load.wait()

    def receive(c, _):
        @pl.when(has_prev)
        def _():
            fwd_copy(c).wait_recv()

        @pl.when(jnp.logical_not(has_prev))
        def _():
            fr[c] = jnp.zeros((TOK, CW), BF16)

        cols = at(c)
        for h in range(2):
            rows = slice(h * HALF, (h + 1) * HALF)
            arrived = rb_v[ids_r[0, h], :, cols].astype(F32)
            next_input[rows, cols] = (arrived + fr[c, rows, :].astype(F32)).astype(BF16)
        return 0

    lax.fori_loop(0, LATE, receive, 0)

    for step in (1, 2, 3):
        z_copy(step, xh, 0).wait_recv()
    x_copy.wait_recv()

    def final(t, _):
        lanes = pl.ds(pl.multiple_of(t * BLOCK, BLOCK), BLOCK)
        mine = pl.ds(pl.multiple_of(d * CW + t * BLOCK, BLOCK), BLOCK)
        gain_row = gain_v[:, mine]
        weighted = jnp.zeros((BLOCK, R), F32)
        for a in range(3):
            rows = slice(a * R, (a + 1) * R)
            total = chip[2 * z + xh, rows, lanes].astype(F32)
            for step in range(3):
                total += z_in[step, xh, rows, lanes].astype(F32)
            total += x_in[rows, lanes].astype(F32)
            if a < 2:
                w_rows = w_v[mine, a * R : (a + 1) * R].astype(F32)
                weighted += w_rows * total.T
                total = total * gain_row
            wgrad[lanes, a * R : (a + 1) * R] = total.T
        ggrad[:, lanes] = jnp.sum(weighted.T, axis=0, keepdims=True)
        return 0

    lax.fori_loop(0, CW // BLOCK, final, 0)
    lax.fori_loop(LATE, NC, receive, 0)

    x_copy.wait_send()

    def drain(c, _):
        @pl.when(has_next)
        def _():
            fwd_copy(c).wait_send()
            bwd_copy(c).wait_recv()

        @pl.when(has_prev)
        def _():
            bwd_copy(c).wait_send()

        return 0

    lax.fori_loop(0, NC, drain, 0)

    def drain_relay(c, _):
        bwd_onward(c).wait_send()
        return 0

    lax.fori_loop(0, fwd_relays + bwd_relays, drain_relay, 0)

    def drain_core(i, _):
        core_copy(i).wait_send()
        return 0

    lax.fori_loop(0, 8, drain_core, 0)
    for step in (1, 2, 3):
        for h in range(2):
            z_copy(step, h, 0).wait_send()


def store(*refs):
    copies = [pltpu.make_async_copy(refs[k], refs[5 + k], refs[10].at[k]) for k in range(5)]
    for c in copies:
        c.start()
    for c in copies:
        c.wait()


def local(
    fwd_input, bwd_input, cotangent, send_buffer, recv_buffer,
    fwd_ids, recv_ids, norm_gain, w_gate, w_in, w_out,
):
    any_spec = pl.BlockSpec(memory_space=pl.ANY)
    smem = pl.BlockSpec(memory_space=pltpu.SMEM)
    dma = pltpu.SemaphoreType.DMA
    wide = (TOK, D)
    chunks = (NC, TOK, CW)
    block = (3 * R, CW)
    outs = pl.pallas_call(
        kernel,
        out_shape=[
            pltpu.VMEM(wide, BF16),
            pltpu.VMEM(wide, BF16),
            pltpu.VMEM(wide, BF16),
            pltpu.VMEM((CW, 3 * R), F32),
            pltpu.VMEM((1, CW), F32),
        ],
        in_specs=[smem, smem] + [any_spec] * 9,
        out_specs=[pl.BlockSpec(memory_space=pltpu.VMEM)] * 5,
        scratch_shapes=[
            pltpu.VMEM(wide, BF16),
            pltpu.VMEM(wide, BF16),
            pltpu.VMEM(wide, BF16),
            pltpu.VMEM((3, HALF, D), BF16),
            pltpu.VMEM((3, HALF, D), BF16),
            pltpu.VMEM((1, D), F32),
            pltpu.VMEM((D, 2 * R), BF16),
            pltpu.VMEM((D, R), BF16),
            pltpu.VMEM((TOK, 2 * R), F32),
            pltpu.VMEM((TOK, 2 * R), F32),
            pltpu.VMEM((TOK, BLOCK), F32),
            pltpu.VMEM((TOK, R), F32),
            pltpu.VMEM((TOK, R), BF16),
            pltpu.VMEM((TOK, 2 * R), BF16),
            pltpu.VMEM((2 * R, TOK), BF16),
            pltpu.VMEM((R, TOK), BF16),
            pltpu.VMEM((TOK, BLOCK), F32),
            pltpu.VMEM(chunks, BF16),
            pltpu.VMEM(chunks, BF16),
            pltpu.VMEM(chunks, BF16),
            pltpu.VMEM((RELAYS, TOK, CW), BF16),
            pltpu.VMEM((NC,) + block, BF16),
            pltpu.VMEM((8,) + block, BF16),
            pltpu.VMEM((8,) + block, BF16),
            pltpu.VMEM((3, 2) + block, BF16),
            pltpu.VMEM(block, BF16),
            pltpu.VMEM(block, BF16),
            dma((6, PIECES)),
            dma((3,)),
            dma((NC,)),
            dma((NC,)),
            dma((NC,)),
            dma((NC,)),
            dma((RELAYS,)),
            dma((RELAYS,)),
            dma((8,)),
            dma((8,)),
            dma((3, 2)),
            dma((3, 2)),
            dma((2,)),
        ],
        compiler_params=pltpu.CompilerParams(
            collective_id=0, has_side_effects=True, vmem_limit_bytes=53 << 20
        ),
        cost_estimate=pl.CostEstimate(
            flops=2 * 11 * TOK * D * R, bytes_accessed=28 << 20, transcendentals=4 * TOK * R
        ),
    )(
        fwd_ids, recv_ids, fwd_input[0], bwd_input[0], cotangent[0], send_buffer[0],
        recv_buffer[0], norm_gain, w_gate[0], w_in[0], w_out[0],
    )
    outs = pl.pallas_call(
        store,
        out_shape=[jax.ShapeDtypeStruct(o.shape, o.dtype) for o in outs],
        in_specs=[pl.BlockSpec(memory_space=pltpu.VMEM)] * 5,
        out_specs=[any_spec] * 5,
        scratch_shapes=[dma((5,))],
        compiler_params=pltpu.CompilerParams(vmem_limit_bytes=2 ** 20),
        cost_estimate=pl.CostEstimate(flops=0, bytes_accessed=7 << 20, transcendentals=0),
    )(*outs)
    return (outs[0][None], outs[1][None], outs[2][None], outs[3][None], outs[4])


def solution(mesh):
    return jax.shard_map(
        local,
        mesh=mesh,
        in_specs=(
            P("section", "dp", None),
            P("section", "dp", None),
            P("section", "dp", None),
            P("section", "dp", None, None),
            P("section", "dp", None, None),
            P("section", "dp"),
            P("section", "dp"),
            P("section", None),
            P("section", None, None),
            P("section", None, None),
            P("section", None, None),
        ),
        out_specs=(
            P("section", "dp", None),
            P("section", "dp", None),
            P("section", "dp", None),
            P("section", "dp", None),
            P("section", "dp"),
        ),
        check_vma=False,
    )
```

```python
import functools

import jax
import jax.numpy as jnp
from jax import lax
from jax.experimental import pallas as pl
from jax.experimental.pallas import tpu as pltpu
from jax.sharding import PartitionSpec as P

MESH = pl.DeviceIdType.MESH
F32 = jnp.float32
BF16 = jnp.bfloat16

BLOCK = 128
EPS_NORM = 1e-05
EPS_SCALE = 1e-06

TOK = 128
HALF = 64
D = 8192
R = 128
CW = 512
NC = D // CW
PIECES = 4
PW = D // PIECES
FIN, BIN, COT, WG, WI, WO, SB = range(7)
RELAYS = 12
SECTIONS = 8
PEERS = 9
LATE = 13


def dot_nn(a, b):
    return jnp.dot(a, b, preferred_element_type=F32)


def dot_nt(a, b):
    return lax.dot_general(a, b, (((1,), (1,)), ((), ())), preferred_element_type=F32)


def at(i):
    return pl.ds(pl.multiple_of(i * CW, CW), CW)


def span(p):
    return pl.ds(pl.multiple_of(p * PW, PW), PW)


def kernel(
    idf, idr, fin, bin_, cot, sbuf, rbuf, gain, wg, wi, wo,
    next_input, send_rows, next_cot, wgrad, ggrad,
    fin_v, bin_v, cot_v, sb_v, rb_v, gain_v, w_v, wo_v,
    acc, acc2, ss, gm, mx, gcat, grad_t, mixed_t, krow,
    fs, fr, bs, relay,
    part, core_in, chip, z_in, x_out, x_in,
    ids_f, ids_r, load_a, load_b, fs_s, fs_r, bs_s, bs_r, rl_s, rl_r, core_s, core_r, z_s, z_r, x_sem,
):
    s = lax.axis_index("section")
    d = lax.axis_index("dp")
    core = lax.rem(d, 2)
    xh = lax.rem(d // 2, 2)
    z = d // 4
    has_next = s < SECTIONS - 1
    has_prev = s > 0

    even = lax.rem(s, 2) == 0

    def piece(kind, p):
        cols = span(p)
        sem = load_a.at[kind, p]
        if kind == FIN:
            return pltpu.make_async_copy(fin.at[:, cols], fin_v.at[:, cols], sem)
        if kind == BIN:
            return pltpu.make_async_copy(bin_.at[:, cols], bin_v.at[:, cols], sem)
        if kind == COT:
            return pltpu.make_async_copy(cot.at[:, cols], cot_v.at[:, cols], sem)
        if kind == WG:
            return pltpu.make_async_copy(wg.at[cols], w_v.at[cols, pl.ds(0, R)], sem)
        if kind == WI:
            return pltpu.make_async_copy(wi.at[cols], w_v.at[cols, pl.ds(R, R)], sem)
        if kind == WO:
            return pltpu.make_async_copy(wo.at[cols], wo_v.at[cols], sem)
        return pltpu.make_async_copy(sbuf.at[:, :, cols], sb_v.at[:, :, cols], sem)

    def start_pieces(*kinds):
        for p in range(PIECES):
            for kind in kinds:
                piece(kind, p).start()

    gain_load = pltpu.make_async_copy(gain, gain_v, load_b.at[0])
    idf_load = pltpu.make_async_copy(idf, ids_f, load_b.at[1])
    idr_load = pltpu.make_async_copy(idr, ids_r, load_b.at[2])
    rb_load = pltpu.make_async_copy(rbuf, rb_v, load_b.at[3])
    gain_load.start()

    @pl.when(even)
    def _():
        start_pieces(FIN, WG, WI)

    @pl.when(jnp.logical_not(even))
    def _():
        start_pieces(BIN, WG, WI)
        start_pieces(COT, WO)

    idf_load.start()
    idr_load.start()

    bar = pltpu.get_barrier_semaphore()

    def greet(to):
        pl.semaphore_signal(bar, inc=1, device_id=to, device_id_type=MESH)

    sibling = (s, d + 1 - 2 * core)
    across = (s, d + 2 - 4 * xh)

    def z_peer(step):
        return (s, lax.rem(z + step, 4) * 4 + xh * 2 + core)

    greet(sibling)
    greet(across)
    for step in (1, 2, 3):
        greet(z_peer(step))

    for step in (1, 2, SECTIONS - 2, SECTIONS - 1):
        greet((lax.rem(s + step, SECTIONS), d))

    gain_load.wait()

    def norm_step(x_ref, p):
        cols = span(p)
        x = x_ref[:, cols].astype(F32)
        xg = (x * gain_v[:, cols]).astype(BF16)
        sq = x * x
        total = sq[:, 0:BLOCK]
        for b in range(1, PW // BLOCK):
            total += sq[:, b * BLOCK : (b + 1) * BLOCK]
        return total, dot_nn(xg, w_v[cols, :])

    fwd_via = jnp.where(jnp.logical_and(jnp.logical_not(even), has_next), 2 * (s + 1), 0)
    bwd_via = jnp.where(jnp.logical_and(even, has_prev), 16 - 2 * s, 0)
    fwd_relays = jnp.where(jnp.logical_not(even), 2 * (s - 1), 0)
    bwd_relays = jnp.where(jnp.logical_and(even, s <= 4), 12 - 2 * s, 0)

    def remote(src, dst, send, recv, to):
        return pltpu.make_async_remote_copy(
            src_ref=src, dst_ref=dst, send_sem=send, recv_sem=recv,
            device_id=(to, d), device_id_type=MESH,
        )

    def fwd_copy(c):
        return remote(fs.at[c], fr.at[c], fs_s, fs_r.at[c], s + 1)

    def fwd_detour(c):
        return remote(fs.at[c], relay.at[c], fs_s, rl_r.at[c], s + 2)

    def fwd_onward(c):
        return remote(relay.at[c], fr.at[c], rl_s.at[c], fs_r.at[c], s - 1)

    def bwd_copy(c):
        return remote(bs.at[c], next_cot.at[:, at(c)], bs_s, bs_r, s - 1)

    def bwd_detour(c):
        return remote(bs.at[c], relay.at[c], bs_s, rl_r.at[c], s - 2)

    def bwd_onward(c):
        return remote(relay.at[c], next_cot.at[:, at(c)], rl_s.at[c], bs_r, s + 1)

    def core_copy(i):
        return pltpu.make_async_remote_copy(
            src_ref=part.at[2 * i + 1 - core], dst_ref=core_in.at[i],
            send_sem=core_s, recv_sem=core_r.at[i],
            device_id=sibling, device_id_type=MESH,
        )

    def forward(first):
        acc[...] = jnp.zeros_like(acc)
        ss[...] = jnp.zeros_like(ss)

        def f1(p, _):
            piece(FIN, p).wait()

            @pl.when(first)
            def _():
                piece(WG, p).wait()
                piece(WI, p).wait()

            @pl.when(jnp.logical_and(first, p == 1))
            def _():
                start_pieces(WO, SB)

            sq, prod = norm_step(fin_v, p)
            ss[...] += sq
            acc[...] += prod
            return 0

        lax.fori_loop(0, PIECES, f1, 0)

        @pl.when(first)
        def _():
            start_pieces(BIN, COT)
            rb_load.start()

        recip = lax.rsqrt(jnp.sum(ss[...], axis=-1, keepdims=True) / D + EPS_NORM)
        gate_pre = acc[:, 0:R] * recip
        inner = acc[:, R : 2 * R] * recip
        mx[...] = (gate_pre * jax.nn.sigmoid(gate_pre) * inner).astype(BF16)

        @pl.when(first)
        def _():
            pl.semaphore_wait(bar, PEERS)

        idf_load.wait()

        def chosen(slot, cols):
            last = jnp.where(slot == 1, sb_v[1, :, cols], sb_v[2, :, cols])
            return jnp.where(slot == 0, sb_v[0, :, cols], last)

        def f2(c, _):
            @pl.when(lax.rem(c, NC // PIECES) == 0)
            def _():
                piece(SB, c // (NC // PIECES)).wait()

                @pl.when(first)
                def _():
                    piece(WO, c // (NC // PIECES)).wait()

            cols = at(c)
            update = dot_nt(mx[...], wo_v[cols, :])
            for h in range(2):
                rows = slice(h * HALF, (h + 1) * HALF)
                stored = chosen(ids_f[0, h], cols).astype(F32)
                diff = fin_v[rows, cols].astype(F32) + update[rows] - stored
                for b in range(CW // BLOCK):
                    lanes = slice(b * BLOCK, (b + 1) * BLOCK)
                    part_diff = diff[:, lanes]
                    top = jnp.max(jnp.abs(part_diff), axis=-1, keepdims=True)
                    scale = (top + EPS_SCALE).astype(BF16).astype(F32)
                    quantized = (part_diff / scale).astype(BF16)
                    product = scale * quantized.astype(F32)
                    fs[c, rows, lanes] = product.astype(BF16)
                    lane_at = pl.ds(pl.multiple_of(c * CW + b * BLOCK, BLOCK), BLOCK)
                    send_rows[rows, lane_at] = (stored[:, lanes] + product).astype(BF16)

            @pl.when(jnp.logical_and(has_next, c >= fwd_via))
            def _():
                fwd_copy(c).start()

            @pl.when(c < fwd_via)
            def _():
                fwd_detour(c).start()

            return 0

        lax.fori_loop(0, NC, f2, 0)

    def backward(first):
        acc2[...] = jnp.zeros_like(acc2)
        ss[...] = jnp.zeros_like(ss)
        gm[...] = jnp.zeros_like(gm)

        def b1(p, _):
            piece(BIN, p).wait()

            @pl.when(first)
            def _():
                piece(WG, p).wait()
                piece(WI, p).wait()

            sq, prod = norm_step(bin_v, p)
            ss[...] += sq
            acc2[...] += prod
            return 0

        lax.fori_loop(0, PIECES, b1, 0)

        def b1_mixed(p, _):
            piece(COT, p).wait()

            @pl.when(first)
            def _():
                piece(WO, p).wait()

            gm[...] += dot_nn(cot_v[:, span(p)], wo_v[span(p), :])
            return 0

        lax.fori_loop(0, PIECES, b1_mixed, 0)

        @pl.when(first)
        def _():
            start_pieces(FIN, SB)
            rb_load.start()

        recip_b = lax.rsqrt(jnp.sum(ss[...], axis=-1, keepdims=True) / D + EPS_NORM)
        gate_b = acc2[:, 0:R] * recip_b
        inner_b = acc2[:, R : 2 * R] * recip_b
        sig = jax.nn.sigmoid(gate_b)
        swish = gate_b * sig
        grad_mixed = gm[...]
        gg = grad_mixed * inner_b * sig * (1.0 + gate_b * (1.0 - sig)) * recip_b
        gi = grad_mixed * swish * recip_b
        gcat[:, 0:R] = gg.astype(BF16)
        gcat[:, R : 2 * R] = gi.astype(BF16)
        grad_t[0:R, :] = gg.T.astype(BF16)
        grad_t[R : 2 * R, :] = gi.T.astype(BF16)
        mixed_t[...] = (swish * inner_b).T.astype(BF16)
        dots = jnp.sum(gg * gate_b + gi * inner_b, axis=-1, keepdims=True)
        krow[...] = jnp.broadcast_to(dots * recip_b * (1.0 / D), (TOK, BLOCK))

        @pl.when(first)
        def _():
            pl.semaphore_wait(bar, PEERS)

        def b2(c, _):
            cols = at(c)
            grad_normed = dot_nt(gcat[...], w_v[cols, :])
            x = bin_v[:, cols].astype(F32)
            for b in range(CW // BLOCK):
                lanes = slice(b * BLOCK, (b + 1) * BLOCK)
                lane_at = pl.ds(pl.multiple_of(c * CW + b * BLOCK, BLOCK), BLOCK)
                passed = (
                    cot_v[:, lane_at].astype(F32)
                    + grad_normed[:, lanes] * gain_v[:, lane_at]
                    - x[:, lanes] * krow[...]
                )
                bs[c, :, lanes] = passed.astype(BF16)

            @pl.when(jnp.logical_and(has_prev, c >= bwd_via))
            def _():
                bwd_copy(c).start()

            @pl.when(c < bwd_via)
            def _():
                bwd_detour(c).start()

            @pl.when(jnp.logical_not(has_next))
            def _():
                next_cot[:, cols] = jnp.zeros((TOK, CW), BF16)

            return 0

        lax.fori_loop(0, NC, b2, 0)

        def b3(j, _):
            cols = at(j)
            part[j, 0 : 2 * R, :] = dot_nn(grad_t[...], bin_v[:, cols]).astype(BF16)
            part[j, 2 * R : 3 * R, :] = dot_nn(mixed_t[...], cot_v[:, cols]).astype(BF16)

            @pl.when(lax.rem(j, 2) != core)
            def _():
                core_copy(j // 2).start()

            return 0

        lax.fori_loop(0, NC, b3, 0)

    def half(turn, _):
        @pl.when(lax.rem(s + turn, 2) == 0)
        def _():
            forward(turn == 0)

        @pl.when(lax.rem(s + turn, 2) == 1)
        def _():
            backward(turn == 0)

        return 0

    lax.fori_loop(0, 2, half, 0)

    def z_copy(step, h, i):
        return pltpu.make_async_remote_copy(
            src_ref=chip.at[i], dst_ref=z_in.at[step - 1, h],
            send_sem=z_s, recv_sem=z_r.at[step - 1, h],
            device_id=z_peer(step), device_id_type=MESH,
        )

    def chip_sum(k, _):
        h = jnp.where(k < 4, 1 - xh, xh)
        step = lax.rem(k + 1, 4)
        i = lax.rem(z + step, 4) * 2 + h
        core_copy(i).wait_recv()

        def rows_sum(t, _):
            rows = pl.ds(pl.multiple_of(t * 64, 64), 64)
            chip[i, rows, :] = (
                part[2 * i + core, rows, :].astype(F32) + core_in[i, rows, :].astype(F32)
            ).astype(BF16)
            return 0

        lax.fori_loop(0, 6, rows_sum, 0)

        @pl.when(step > 0)
        def _():
            z_copy(step, h, i).start()

        return 0

    lax.fori_loop(0, 8, chip_sum, 0)

    def hand_on(c, _):
        @pl.when(even)
        def _():
            bwd_detour(c).wait_recv()
            bwd_onward(c).start()

        @pl.when(jnp.logical_not(even))
        def _():
            fwd_detour(c).wait_recv()
            fwd_onward(c).start()

        return 0

    lax.fori_loop(0, fwd_relays + bwd_relays, hand_on, 0)

    x_copy = pltpu.make_async_remote_copy(
        src_ref=x_out, dst_ref=x_in, send_sem=x_sem.at[0], recv_sem=x_sem.at[1],
        device_id=across, device_id_type=MESH,
    )

    def z_sum(h, rows):
        total = chip[2 * z + h, rows, :].astype(F32)
        for step in range(3):
            total += z_in[step, h, rows, :].astype(F32)
        return total

    for step in (1, 2, 3):
        z_copy(step, 1 - xh, 0).wait_recv()

    def other_sum(t, _):
        rows = pl.ds(pl.multiple_of(t * 64, 64), 64)
        x_out[rows, :] = z_sum(1 - xh, rows).astype(BF16)
        return 0

    lax.fori_loop(0, 6, other_sum, 0)
    x_copy.start()

    fwd_late = jnp.where(even, 2 * s, 0)
    rb_load.wait()
    idr_load.wait()

    def receive(k, _):
        c = lax.rem(k + fwd_late, NC)

        @pl.when(has_prev)
        def _():
            fwd_copy(c).wait_recv()

        @pl.when(jnp.logical_not(has_prev))
        def _():
            fr[c] = jnp.zeros((TOK, CW), BF16)

        cols = at(c)
        for h in range(2):
            rows = slice(h * HALF, (h + 1) * HALF)
            arrived = rb_v[ids_r[0, h], :, cols].astype(F32)
            next_input[rows, cols] = (arrived + fr[c, rows, :].astype(F32)).astype(BF16)
        return 0

    lax.fori_loop(0, LATE, receive, 0)

    for step in (1, 2, 3):
        z_copy(step, xh, 0).wait_recv()
    x_copy.wait_recv()

    def final(t, _):
        lanes = pl.ds(pl.multiple_of(t * BLOCK, BLOCK), BLOCK)
        mine = pl.ds(pl.multiple_of(d * CW + t * BLOCK, BLOCK), BLOCK)
        gain_row = gain_v[:, mine]
        weighted = jnp.zeros((BLOCK, R), F32)
        for a in range(3):
            rows = slice(a * R, (a + 1) * R)
            total = chip[2 * z + xh, rows, lanes].astype(F32)
            for step in range(3):
                total += z_in[step, xh, rows, lanes].astype(F32)
            total += x_in[rows, lanes].astype(F32)
            if a < 2:
                w_rows = w_v[mine, a * R : (a + 1) * R].astype(F32)
                weighted += w_rows * total.T
                total = total * gain_row
            wgrad[lanes, a * R : (a + 1) * R] = total.T
        ggrad[:, lanes] = jnp.sum(weighted.T, axis=0, keepdims=True)
        return 0

    lax.fori_loop(0, CW // BLOCK, final, 0)
    lax.fori_loop(LATE, NC, receive, 0)

    x_copy.wait_send()

    def ended(src, send):
        pltpu.make_async_copy(src, src, send).wait()

    ended(part.at[pl.ds(0, 8)], core_s)
    ended(part.at[pl.ds(0, 6)], z_s)

    def drain_relay(c, _):
        bwd_onward(c).wait_send()
        return 0

    @pl.when(has_next)
    def _():
        ended(fs, fs_s)

    lax.fori_loop(0, fwd_relays + bwd_relays, drain_relay, 0)

    @pl.when(has_prev)
    def _():
        ended(bs, bs_s)

    @pl.when(has_next)
    def _():
        ended(next_cot, bs_r)


def store(*refs):
    copies = [pltpu.make_async_copy(refs[k], refs[5 + k], refs[10].at[k]) for k in range(5)]
    for c in copies:
        c.start()
    for c in copies:
        c.wait()


def local(
    fwd_input, bwd_input, cotangent, send_buffer, recv_buffer,
    fwd_ids, recv_ids, norm_gain, w_gate, w_in, w_out,
):
    any_spec = pl.BlockSpec(memory_space=pl.ANY)
    dma = pltpu.SemaphoreType.DMA
    wide = (TOK, D)
    chunks = (NC, TOK, CW)
    block = (3 * R, CW)
    outs = pl.pallas_call(
        kernel,
        out_shape=[
            pltpu.VMEM(wide, BF16),
            pltpu.VMEM(wide, BF16),
            pltpu.VMEM(wide, BF16),
            pltpu.VMEM((CW, 3 * R), F32),
            pltpu.VMEM((1, CW), F32),
        ],
        in_specs=[any_spec] * 11,
        out_specs=[pl.BlockSpec(memory_space=pltpu.VMEM)] * 5,
        scratch_shapes=[
            pltpu.VMEM(wide, BF16),
            pltpu.VMEM(wide, BF16),
            pltpu.VMEM(wide, BF16),
            pltpu.VMEM((3, HALF, D), BF16),
            pltpu.VMEM((3, HALF, D), BF16),
            pltpu.VMEM((1, D), F32),
            pltpu.VMEM((D, 2 * R), BF16),
            pltpu.VMEM((D, R), BF16),
            pltpu.VMEM((TOK, 2 * R), F32),
            pltpu.VMEM((TOK, 2 * R), F32),
            pltpu.VMEM((TOK, BLOCK), F32),
            pltpu.VMEM((TOK, R), F32),
            pltpu.VMEM((TOK, R), BF16),
            pltpu.VMEM((TOK, 2 * R), BF16),
            pltpu.VMEM((2 * R, TOK), BF16),
            pltpu.VMEM((R, TOK), BF16),
            pltpu.VMEM((TOK, BLOCK), F32),
            pltpu.VMEM(chunks, BF16),
            pltpu.VMEM(chunks, BF16),
            pltpu.VMEM(chunks, BF16),
            pltpu.VMEM((RELAYS, TOK, CW), BF16),
            pltpu.VMEM((NC,) + block, BF16),
            pltpu.VMEM((8,) + block, BF16),
            pltpu.VMEM((8,) + block, BF16),
            pltpu.VMEM((3, 2) + block, BF16),
            pltpu.VMEM(block, BF16),
            pltpu.VMEM(block, BF16),
            pltpu.SMEM((1, 2), jnp.int32),
            pltpu.SMEM((1, 2), jnp.int32),
            dma((7, PIECES)),
            dma((4,)),
            dma,
            dma((NC,)),
            dma,
            dma,
            dma((RELAYS,)),
            dma((RELAYS,)),
            dma,
            dma((8,)),
            dma,
            dma((3, 2)),
            dma((2,)),
        ],
        compiler_params=pltpu.CompilerParams(
            collective_id=0, has_side_effects=True, vmem_limit_bytes=53 << 20
        ),
        cost_estimate=pl.CostEstimate(
            flops=2 * 11 * TOK * D * R, bytes_accessed=28 << 20, transcendentals=4 * TOK * R
        ),
    )(
        fwd_ids, recv_ids, fwd_input[0], bwd_input[0], cotangent[0], send_buffer[0],
        recv_buffer[0], norm_gain, w_gate[0], w_in[0], w_out[0],
    )
    outs = pl.pallas_call(
        store,
        out_shape=[jax.ShapeDtypeStruct(o.shape, o.dtype) for o in outs],
        in_specs=[pl.BlockSpec(memory_space=pltpu.VMEM)] * 5,
        out_specs=[any_spec] * 5,
        scratch_shapes=[dma((5,))],
        compiler_params=pltpu.CompilerParams(vmem_limit_bytes=2 ** 20),
        cost_estimate=pl.CostEstimate(flops=0, bytes_accessed=7 << 20, transcendentals=0),
    )(*outs)
    return (outs[0][None], outs[1][None], outs[2][None], outs[3][None], outs[4])


def solution(mesh):
    return jax.shard_map(
        local,
        mesh=mesh,
        in_specs=(
            P("section", "dp", None),
            P("section", "dp", None),
            P("section", "dp", None),
            P("section", "dp", None, None),
            P("section", "dp", None, None),
            P("section", "dp"),
            P("section", "dp"),
            P("section", None),
            P("section", None, None),
            P("section", None, None),
            P("section", None, None),
        ),
        out_specs=(
            P("section", "dp", None),
            P("section", "dp", None),
            P("section", "dp", None),
            P("section", "dp", None),
            P("section", "dp"),
        ),
        check_vma=False,
    )
```

```python
import functools

import jax
import jax.numpy as jnp
from jax import lax
from jax.experimental import pallas as pl
from jax.experimental.pallas import tpu as pltpu
from jax.sharding import PartitionSpec as P

MESH = pl.DeviceIdType.MESH
F32 = jnp.float32
BF16 = jnp.bfloat16

BLOCK = 128
EPS_NORM = 1e-05
EPS_SCALE = 1e-06

TOK = 128
HALF = 64
D = 8192
R = 128
CW = 512
NC = D // CW
PIECES = 4
PW = D // PIECES
FIN, BIN, COT, WG, WI, WO, SB = range(7)
RELAYS = 12
SECTIONS = 8
PEERS = 9
HELD = 12
LATE = 9


def dot_nn(a, b):
    return jnp.dot(a, b, preferred_element_type=F32)


def dot_nt(a, b):
    return lax.dot_general(a, b, (((1,), (1,)), ((), ())), preferred_element_type=F32)


def at(i):
    return pl.ds(pl.multiple_of(i * CW, CW), CW)


def span(p):
    return pl.ds(pl.multiple_of(p * PW, PW), PW)


def kernel(
    idf, idr, fin, bin_, cot, sbuf, rbuf, gain, wg, wi, wo,
    next_input, send_rows, next_cot, wgrad, ggrad,
    fin_v, bin_v, cot_v, sb_v, rb_v, gain_v, w_v, wo_v,
    acc, acc2, ss, gm, mx, gcat, grad_t, mixed_t, krow,
    fs, fr, bs, relay,
    part, core_in, chip, z_in, x_out, x_in,
    ids_f, ids_r, load_a, load_b, fs_s, fs_r, bs_s, bs_r, rl_s, rl_r, core_s, core_r, z_s, z_r, x_sem,
):
    s = lax.axis_index("section")
    d = lax.axis_index("dp")
    core = lax.rem(d, 2)
    xh = lax.rem(d // 2, 2)
    z = d // 4
    has_next = s < SECTIONS - 1
    has_prev = s > 0

    even = lax.rem(s, 2) == 0

    def piece(kind, p):
        cols = span(p)
        sem = load_a.at[kind, p]
        if kind == FIN:
            return pltpu.make_async_copy(fin.at[:, cols], fin_v.at[:, cols], sem)
        if kind == BIN:
            return pltpu.make_async_copy(bin_.at[:, cols], bin_v.at[:, cols], sem)
        if kind == COT:
            return pltpu.make_async_copy(cot.at[:, cols], cot_v.at[:, cols], sem)
        if kind == WG:
            return pltpu.make_async_copy(wg.at[cols], w_v.at[cols, pl.ds(0, R)], sem)
        if kind == WI:
            return pltpu.make_async_copy(wi.at[cols], w_v.at[cols, pl.ds(R, R)], sem)
        if kind == WO:
            return pltpu.make_async_copy(wo.at[cols], wo_v.at[cols], sem)
        return pltpu.make_async_copy(sbuf.at[:, :, cols], sb_v.at[:, :, cols], sem)

    def start_pieces(*kinds):
        for p in range(PIECES):
            for kind in kinds:
                piece(kind, p).start()

    gain_load = pltpu.make_async_copy(gain, gain_v, load_b.at[0])
    idf_load = pltpu.make_async_copy(idf, ids_f, load_b.at[1])
    idr_load = pltpu.make_async_copy(idr, ids_r, load_b.at[2])
    rb_load = pltpu.make_async_copy(rbuf, rb_v, load_b.at[3])
    gain_load.start()

    @pl.when(even)
    def _():
        start_pieces(FIN, WG, WI)

    @pl.when(jnp.logical_not(even))
    def _():
        start_pieces(BIN, WG, WI, COT, WO)

    idf_load.start()
    idr_load.start()

    bar = pltpu.get_barrier_semaphore()

    def greet(to):
        pl.semaphore_signal(bar, inc=1, device_id=to, device_id_type=MESH)

    sibling = (s, d + 1 - 2 * core)
    across = (s, d + 2 - 4 * xh)

    def z_peer(step):
        return (s, lax.rem(z + step, 4) * 4 + xh * 2 + core)

    greet(sibling)
    greet(across)
    for step in (1, 2, 3):
        greet(z_peer(step))

    for step in (1, 2, SECTIONS - 2, SECTIONS - 1):
        greet((lax.rem(s + step, SECTIONS), d))

    gain_load.wait()

    def norm_step(x_ref, p):
        cols = span(p)
        x = x_ref[:, cols].astype(F32)
        xg = (x * gain_v[:, cols]).astype(BF16)
        sq = x * x
        total = sq[:, 0:BLOCK]
        for b in range(1, PW // BLOCK):
            total += sq[:, b * BLOCK : (b + 1) * BLOCK]
        return total, dot_nn(xg, w_v[cols, :])

    fwd_via = jnp.where(jnp.logical_and(jnp.logical_not(even), has_next), 2 * (s + 1), 0)
    bwd_via = jnp.where(jnp.logical_and(even, has_prev), 16 - 2 * s, 0)
    fwd_relays = jnp.where(jnp.logical_not(even), 2 * (s - 1), 0)
    bwd_relays = jnp.where(jnp.logical_and(even, s <= 4), 12 - 2 * s, 0)

    def remote(src, dst, send, recv, to):
        return pltpu.make_async_remote_copy(
            src_ref=src, dst_ref=dst, send_sem=send, recv_sem=recv,
            device_id=(to, d), device_id_type=MESH,
        )

    def fwd_copy(c):
        return remote(fs.at[c], fr.at[c], fs_s, fs_r.at[c], s + 1)

    def fwd_detour(c):
        return remote(fs.at[c], relay.at[c], fs_s, rl_r.at[c], s + 2)

    def fwd_onward(c):
        return remote(relay.at[c], fr.at[c], rl_s.at[c], fs_r.at[c], s - 1)

    def bwd_copy(c):
        return remote(bs.at[c], next_cot.at[:, at(c)], bs_s, bs_r, s - 1)

    def bwd_detour(c):
        return remote(bs.at[c], relay.at[c], bs_s, rl_r.at[c], s - 2)

    def bwd_onward(c):
        return remote(relay.at[c], next_cot.at[:, at(c)], rl_s.at[c], bs_r, s + 1)

    def core_copy(i):
        return pltpu.make_async_remote_copy(
            src_ref=part.at[2 * i + 1 - core], dst_ref=core_in.at[i],
            send_sem=core_s, recv_sem=core_r.at[i],
            device_id=sibling, device_id_type=MESH,
        )

    def forward(first):
        acc[...] = jnp.zeros_like(acc)
        ss[...] = jnp.zeros_like(ss)

        def f1(p, _):
            piece(FIN, p).wait()

            @pl.when(first)
            def _():
                piece(WG, p).wait()
                piece(WI, p).wait()

            @pl.when(jnp.logical_and(first, p == 1))
            def _():
                start_pieces(WO, SB)

            sq, prod = norm_step(fin_v, p)
            ss[...] += sq
            acc[...] += prod
            return 0

        lax.fori_loop(0, PIECES, f1, 0)

        @pl.when(first)
        def _():
            start_pieces(BIN, COT)
            rb_load.start()

        recip = lax.rsqrt(jnp.sum(ss[...], axis=-1, keepdims=True) / D + EPS_NORM)
        gate_pre = acc[:, 0:R] * recip
        inner = acc[:, R : 2 * R] * recip
        mx[...] = (gate_pre * jax.nn.sigmoid(gate_pre) * inner).astype(BF16)

        @pl.when(first)
        def _():
            pl.semaphore_wait(bar, PEERS)

        idf_load.wait()

        def chosen(slot, cols):
            last = jnp.where(slot == 1, sb_v[1, :, cols], sb_v[2, :, cols])
            return jnp.where(slot == 0, sb_v[0, :, cols], last)

        def f2(c, _):
            @pl.when(lax.rem(c, NC // PIECES) == 0)
            def _():
                piece(SB, c // (NC // PIECES)).wait()

                @pl.when(first)
                def _():
                    piece(WO, c // (NC // PIECES)).wait()

            cols = at(c)
            update = dot_nt(mx[...], wo_v[cols, :])
            for h in range(2):
                rows = slice(h * HALF, (h + 1) * HALF)
                stored = chosen(ids_f[0, h], cols).astype(F32)
                diff = fin_v[rows, cols].astype(F32) + update[rows] - stored
                for b in range(CW // BLOCK):
                    lanes = slice(b * BLOCK, (b + 1) * BLOCK)
                    part_diff = diff[:, lanes]
                    top = jnp.max(jnp.abs(part_diff), axis=-1, keepdims=True)
                    scale = (top + EPS_SCALE).astype(BF16).astype(F32)
                    quantized = (part_diff / scale).astype(BF16)
                    product = scale * quantized.astype(F32)
                    fs[c, rows, lanes] = product.astype(BF16)
                    lane_at = pl.ds(pl.multiple_of(c * CW + b * BLOCK, BLOCK), BLOCK)
                    send_rows[rows, lane_at] = (stored[:, lanes] + product).astype(BF16)

            @pl.when(jnp.logical_and(has_next, jnp.logical_and(c >= fwd_via, jnp.logical_or(even, c < HELD))))
            def _():
                fwd_copy(c).start()

            @pl.when(c < fwd_via)
            def _():
                fwd_detour(c).start()

            return 0

        lax.fori_loop(0, NC, f2, 0)

    def backward(first):
        acc2[...] = jnp.zeros_like(acc2)
        ss[...] = jnp.zeros_like(ss)
        gm[...] = jnp.zeros_like(gm)

        def b1(p, _):
            piece(BIN, p).wait()
            piece(COT, p).wait()

            @pl.when(first)
            def _():
                for kind in (WG, WI, WO):
                    piece(kind, p).wait()

            sq, prod = norm_step(bin_v, p)
            mixed_prod = dot_nn(cot_v[:, span(p)], wo_v[span(p), :])
            ss[...] += sq
            acc2[...] += prod
            gm[...] += mixed_prod
            return 0

        lax.fori_loop(0, PIECES, b1, 0)

        @pl.when(first)
        def _():
            start_pieces(FIN, SB)
            rb_load.start()

        recip_b = lax.rsqrt(jnp.sum(ss[...], axis=-1, keepdims=True) / D + EPS_NORM)
        gate_b = acc2[:, 0:R] * recip_b
        inner_b = acc2[:, R : 2 * R] * recip_b
        sig = jax.nn.sigmoid(gate_b)
        swish = gate_b * sig
        grad_mixed = gm[...]
        gg = grad_mixed * inner_b * sig * (1.0 + gate_b * (1.0 - sig)) * recip_b
        gi = grad_mixed * swish * recip_b
        gcat[:, 0:R] = gg.astype(BF16)
        gcat[:, R : 2 * R] = gi.astype(BF16)
        acc2[:, 0:R] = gg
        acc2[:, R : 2 * R] = gi
        gm[...] = swish * inner_b
        dots = jnp.sum(gg * gate_b + gi * inner_b, axis=-1, keepdims=True)
        krow[...] = jnp.broadcast_to(dots * recip_b * (1.0 / D), (TOK, BLOCK))

        @pl.when(first)
        def _():
            pl.semaphore_wait(bar, PEERS)

        def b2(c, _):
            cols = at(c)
            grad_normed = dot_nt(gcat[...], w_v[cols, :])
            x = bin_v[:, cols].astype(F32)
            for b in range(CW // BLOCK):
                lanes = slice(b * BLOCK, (b + 1) * BLOCK)
                lane_at = pl.ds(pl.multiple_of(c * CW + b * BLOCK, BLOCK), BLOCK)
                passed = (
                    cot_v[:, lane_at].astype(F32)
                    + grad_normed[:, lanes] * gain_v[:, lane_at]
                    - x[:, lanes] * krow[...]
                )
                bs[c, :, lanes] = passed.astype(BF16)

            @pl.when(jnp.logical_and(has_prev, jnp.logical_and(c >= bwd_via, jnp.logical_or(jnp.logical_not(even), c < HELD))))
            def _():
                bwd_copy(c).start()

            @pl.when(c < bwd_via)
            def _():
                bwd_detour(c).start()

            @pl.when(jnp.logical_not(has_next))
            def _():
                next_cot[:, cols] = jnp.zeros((TOK, CW), BF16)

            return 0

        lax.fori_loop(0, NC, b2, 0)

        grad_t[0:R, :] = acc2[:, 0:R].T.astype(BF16)
        grad_t[R : 2 * R, :] = acc2[:, R : 2 * R].T.astype(BF16)
        mixed_t[...] = gm[...].T.astype(BF16)

        def b3(j, _):
            cols = at(j)
            part[j, 0 : 2 * R, :] = dot_nn(grad_t[...], bin_v[:, cols]).astype(BF16)
            part[j, 2 * R : 3 * R, :] = dot_nn(mixed_t[...], cot_v[:, cols]).astype(BF16)

            @pl.when(lax.rem(j, 2) != core)
            def _():
                core_copy(j // 2).start()

            return 0

        lax.fori_loop(0, NC, b3, 0)

    def half(turn, _):
        @pl.when(lax.rem(s + turn, 2) == 0)
        def _():
            forward(turn == 0)

        @pl.when(lax.rem(s + turn, 2) == 1)
        def _():
            backward(turn == 0)

        return 0

    lax.fori_loop(0, 2, half, 0)

    def z_copy(step, h, i):
        return pltpu.make_async_remote_copy(
            src_ref=chip.at[i], dst_ref=z_in.at[step - 1, h],
            send_sem=z_s, recv_sem=z_r.at[step - 1, h],
            device_id=z_peer(step), device_id_type=MESH,
        )

    def chip_sum(k, _):
        h = jnp.where(k < 4, 1 - xh, xh)
        step = lax.rem(k + 1, 4)
        i = lax.rem(z + step, 4) * 2 + h
        core_copy(i).wait_recv()

        def rows_sum(t, _):
            rows = pl.ds(pl.multiple_of(t * 64, 64), 64)
            chip[i, rows, :] = (
                part[2 * i + core, rows, :].astype(F32) + core_in[i, rows, :].astype(F32)
            ).astype(BF16)
            return 0

        lax.fori_loop(0, 6, rows_sum, 0)

        @pl.when(step > 0)
        def _():
            z_copy(step, h, i).start()

        return 0

    lax.fori_loop(0, 8, chip_sum, 0)

    def hand_on(c, _):
        @pl.when(even)
        def _():
            bwd_detour(c).wait_recv()
            bwd_onward(c).start()

        @pl.when(jnp.logical_not(even))
        def _():
            fwd_detour(c).wait_recv()
            fwd_onward(c).start()

        return 0

    relays = fwd_relays + bwd_relays
    lax.fori_loop(0, relays - 4, hand_on, 0)

    x_copy = pltpu.make_async_remote_copy(
        src_ref=x_out, dst_ref=x_in, send_sem=x_sem.at[0], recv_sem=x_sem.at[1],
        device_id=across, device_id_type=MESH,
    )

    def z_sum(h, rows):
        total = chip[2 * z + h, rows, :].astype(F32)
        for step in range(3):
            total += z_in[step, h, rows, :].astype(F32)
        return total

    for step in (1, 2, 3):
        z_copy(step, 1 - xh, 0).wait_recv()

    def other_sum(t, _):
        rows = pl.ds(pl.multiple_of(t * 64, 64), 64)
        x_out[rows, :] = z_sum(1 - xh, rows).astype(BF16)
        return 0

    lax.fori_loop(0, 6, other_sum, 0)
    x_copy.start()

    def send_held(c, _):
        @pl.when(jnp.logical_and(even, has_prev))
        def _():
            bwd_copy(c).start()

        @pl.when(jnp.logical_and(jnp.logical_not(even), has_next))
        def _():
            fwd_copy(c).start()

        return 0

    lax.fori_loop(HELD, NC, send_held, 0)
    lax.fori_loop(jnp.maximum(relays - 4, 0), relays, hand_on, 0)

    fwd_late = jnp.where(even, 2 * s, 0)
    rb_load.wait()
    idr_load.wait()

    def receive(k, _):
        c = lax.rem(k + fwd_late, NC)

        @pl.when(has_prev)
        def _():
            fwd_copy(c).wait_recv()

        @pl.when(jnp.logical_not(has_prev))
        def _():
            fr[c] = jnp.zeros((TOK, CW), BF16)

        cols = at(c)
        for h in range(2):
            rows = slice(h * HALF, (h + 1) * HALF)
            arrived = rb_v[ids_r[0, h], :, cols].astype(F32)
            next_input[rows, cols] = (arrived + fr[c, rows, :].astype(F32)).astype(BF16)
        return 0

    lax.fori_loop(0, LATE, receive, 0)

    for step in (1, 2, 3):
        z_copy(step, xh, 0).wait_recv()
    x_copy.wait_recv()

    def final(t, _):
        lanes = pl.ds(pl.multiple_of(t * BLOCK, BLOCK), BLOCK)
        mine = pl.ds(pl.multiple_of(d * CW + t * BLOCK, BLOCK), BLOCK)
        gain_row = gain_v[:, mine]
        weighted = jnp.zeros((BLOCK, R), F32)
        for a in range(3):
            rows = slice(a * R, (a + 1) * R)
            total = chip[2 * z + xh, rows, lanes].astype(F32)
            for step in range(3):
                total += z_in[step, xh, rows, lanes].astype(F32)
            total += x_in[rows, lanes].astype(F32)
            if a < 2:
                w_rows = w_v[mine, a * R : (a + 1) * R].astype(F32)
                weighted += w_rows * total.T
                total = total * gain_row
            wgrad[lanes, a * R : (a + 1) * R] = total.T
        ggrad[:, lanes] = jnp.sum(weighted.T, axis=0, keepdims=True)
        return 0

    lax.fori_loop(0, CW // BLOCK, final, 0)
    lax.fori_loop(LATE, NC, receive, 0)

    x_copy.wait_send()

    def ended(src, send):
        pltpu.make_async_copy(src, src, send).wait()

    ended(part.at[pl.ds(0, 8)], core_s)
    ended(part.at[pl.ds(0, 6)], z_s)

    def drain_relay(c, _):
        bwd_onward(c).wait_send()
        return 0

    @pl.when(has_next)
    def _():
        ended(fs, fs_s)

    lax.fori_loop(0, relays, drain_relay, 0)

    @pl.when(has_prev)
    def _():
        ended(bs, bs_s)

    @pl.when(has_next)
    def _():
        ended(next_cot, bs_r)


def store(*refs):
    copies = [pltpu.make_async_copy(refs[k], refs[5 + k], refs[10].at[k]) for k in range(5)]
    for c in copies:
        c.start()
    for c in copies:
        c.wait()


def local(
    fwd_input, bwd_input, cotangent, send_buffer, recv_buffer,
    fwd_ids, recv_ids, norm_gain, w_gate, w_in, w_out,
):
    any_spec = pl.BlockSpec(memory_space=pl.ANY)
    dma = pltpu.SemaphoreType.DMA
    wide = (TOK, D)
    chunks = (NC, TOK, CW)
    block = (3 * R, CW)
    outs = pl.pallas_call(
        kernel,
        out_shape=[
            pltpu.VMEM(wide, BF16),
            pltpu.VMEM(wide, BF16),
            pltpu.VMEM(wide, BF16),
            pltpu.VMEM((CW, 3 * R), F32),
            pltpu.VMEM((1, CW), F32),
        ],
        in_specs=[any_spec] * 11,
        out_specs=[pl.BlockSpec(memory_space=pltpu.VMEM)] * 5,
        scratch_shapes=[
            pltpu.VMEM(wide, BF16),
            pltpu.VMEM(wide, BF16),
            pltpu.VMEM(wide, BF16),
            pltpu.VMEM((3, HALF, D), BF16),
            pltpu.VMEM((3, HALF, D), BF16),
            pltpu.VMEM((1, D), F32),
            pltpu.VMEM((D, 2 * R), BF16),
            pltpu.VMEM((D, R), BF16),
            pltpu.VMEM((TOK, 2 * R), F32),
            pltpu.VMEM((TOK, 2 * R), F32),
            pltpu.VMEM((TOK, BLOCK), F32),
            pltpu.VMEM((TOK, R), F32),
            pltpu.VMEM((TOK, R), BF16),
            pltpu.VMEM((TOK, 2 * R), BF16),
            pltpu.VMEM((2 * R, TOK), BF16),
            pltpu.VMEM((R, TOK), BF16),
            pltpu.VMEM((TOK, BLOCK), F32),
            pltpu.VMEM(chunks, BF16),
            pltpu.VMEM(chunks, BF16),
            pltpu.VMEM(chunks, BF16),
            pltpu.VMEM((RELAYS, TOK, CW), BF16),
            pltpu.VMEM((NC,) + block, BF16),
            pltpu.VMEM((8,) + block, BF16),
            pltpu.VMEM((8,) + block, BF16),
            pltpu.VMEM((3, 2) + block, BF16),
            pltpu.VMEM(block, BF16),
            pltpu.VMEM(block, BF16),
            pltpu.SMEM((1, 2), jnp.int32),
            pltpu.SMEM((1, 2), jnp.int32),
            dma((7, PIECES)),
            dma((4,)),
            dma,
            dma((NC,)),
            dma,
            dma,
            dma((RELAYS,)),
            dma((RELAYS,)),
            dma,
            dma((8,)),
            dma,
            dma((3, 2)),
            dma((2,)),
        ],
        compiler_params=pltpu.CompilerParams(
            collective_id=0, has_side_effects=True, vmem_limit_bytes=53 << 20
        ),
        cost_estimate=pl.CostEstimate(
            flops=2 * 11 * TOK * D * R, bytes_accessed=28 << 20, transcendentals=4 * TOK * R
        ),
    )(
        fwd_ids, recv_ids, fwd_input[0], bwd_input[0], cotangent[0], send_buffer[0],
        recv_buffer[0], norm_gain, w_gate[0], w_in[0], w_out[0],
    )
    outs = pl.pallas_call(
        store,
        out_shape=[jax.ShapeDtypeStruct(o.shape, o.dtype) for o in outs],
        in_specs=[pl.BlockSpec(memory_space=pltpu.VMEM)] * 5,
        out_specs=[any_spec] * 5,
        scratch_shapes=[dma((5,))],
        compiler_params=pltpu.CompilerParams(vmem_limit_bytes=2 ** 20),
        cost_estimate=pl.CostEstimate(flops=0, bytes_accessed=7 << 20, transcendentals=0),
    )(*outs)
    return (outs[0][None], outs[1][None], outs[2][None], outs[3][None], outs[4])


def solution(mesh):
    return jax.shard_map(
        local,
        mesh=mesh,
        in_specs=(
            P("section", "dp", None),
            P("section", "dp", None),
            P("section", "dp", None),
            P("section", "dp", None, None),
            P("section", "dp", None, None),
            P("section", "dp"),
            P("section", "dp"),
            P("section", None),
            P("section", None, None),
            P("section", None, None),
            P("section", None, None),
        ),
        out_specs=(
            P("section", "dp", None),
            P("section", "dp", None),
            P("section", "dp", None),
            P("section", "dp", None),
            P("section", "dp"),
        ),
        check_vma=False,
    )
```

```python
import functools

import jax
import jax.numpy as jnp
from jax import lax
from jax.experimental import pallas as pl
from jax.experimental.pallas import tpu as pltpu
from jax.sharding import PartitionSpec as P

MESH = pl.DeviceIdType.MESH
F32 = jnp.float32
BF16 = jnp.bfloat16

BLOCK = 128
EPS_NORM = 1e-05
EPS_SCALE = 1e-06

TOK = 128
HALF = 64
D = 8192
R = 128
CW = 512
NC = D // CW
PIECES = 8
PW = D // PIECES
FIN, BIN, COT, WG, WI, WO, SB = range(7)
RELAYS = 12
SECTIONS = 8
PEERS = 9
HELD = 13
LATE = 9


def dot_nn(a, b):
    return jnp.dot(a, b, preferred_element_type=F32)


def dot_nt(a, b):
    return lax.dot_general(a, b, (((1,), (1,)), ((), ())), preferred_element_type=F32)


def at(i):
    return pl.ds(pl.multiple_of(i * CW, CW), CW)


def span(p):
    return pl.ds(pl.multiple_of(p * PW, PW), PW)


def kernel(
    idf, idr, fin, bin_, cot, sbuf, rbuf, gain, wg, wi, wo,
    next_input, send_rows, next_cot, wgrad, ggrad,
    fin_v, bin_v, cot_v, sb_v, rb_v, gain_v, w_v, wo_v,
    acc, acc2, ss, gm, mx, gcat, grad_t, mixed_t, krow,
    fs, fr, bs, relay,
    part, core_in, chip, z_in, x_out, x_in,
    ids_f, ids_r, load_a, load_b, fs_s, fs_r, bs_s, bs_r, rl_s, rl_r, core_s, core_r, z_s, z_r, x_sem,
):
    s = lax.axis_index("section")
    d = lax.axis_index("dp")
    core = lax.rem(d, 2)
    xh = lax.rem(d // 2, 2)
    z = d // 4
    has_next = s < SECTIONS - 1
    has_prev = s > 0

    even = lax.rem(s, 2) == 0

    def piece(kind, p):
        cols = span(p)
        sem = load_a.at[kind, p]
        if kind == FIN:
            return pltpu.make_async_copy(fin.at[:, cols], fin_v.at[:, cols], sem)
        if kind == BIN:
            return pltpu.make_async_copy(bin_.at[:, cols], bin_v.at[:, cols], sem)
        if kind == COT:
            return pltpu.make_async_copy(cot.at[:, cols], cot_v.at[:, cols], sem)
        if kind == WG:
            return pltpu.make_async_copy(wg.at[cols], w_v.at[cols, pl.ds(0, R)], sem)
        if kind == WI:
            return pltpu.make_async_copy(wi.at[cols], w_v.at[cols, pl.ds(R, R)], sem)
        if kind == WO:
            return pltpu.make_async_copy(wo.at[cols], wo_v.at[cols], sem)
        return pltpu.make_async_copy(sbuf.at[:, :, cols], sb_v.at[:, :, cols], sem)

    def start_pieces(*kinds):
        for p in range(PIECES):
            for kind in kinds:
                piece(kind, p).start()

    gain_load = pltpu.make_async_copy(gain, gain_v, load_b.at[0])
    idf_load = pltpu.make_async_copy(idf, ids_f, load_b.at[1])
    idr_load = pltpu.make_async_copy(idr, ids_r, load_b.at[2])
    rb_load = pltpu.make_async_copy(rbuf, rb_v, load_b.at[3])
    gain_load.start()

    @pl.when(even)
    def _():
        start_pieces(FIN, WG, WI)

    @pl.when(jnp.logical_not(even))
    def _():
        start_pieces(BIN, WG, WI, COT, WO)

    idf_load.start()
    idr_load.start()

    bar = pltpu.get_barrier_semaphore()

    def greet(to):
        pl.semaphore_signal(bar, inc=1, device_id=to, device_id_type=MESH)

    sibling = (s, d + 1 - 2 * core)
    across = (s, d + 2 - 4 * xh)

    def z_peer(step):
        return (s, lax.rem(z + step, 4) * 4 + xh * 2 + core)

    greet(sibling)
    greet(across)
    for step in (1, 2, 3):
        greet(z_peer(step))

    for step in (1, 2, SECTIONS - 2, SECTIONS - 1):
        greet((lax.rem(s + step, SECTIONS), d))

    gain_load.wait()

    def norm_step(x_ref, p):
        cols = span(p)
        x = x_ref[:, cols].astype(F32)
        xg = (x * gain_v[:, cols]).astype(BF16)
        sq = x * x
        total = sq[:, 0:BLOCK]
        for b in range(1, PW // BLOCK):
            total += sq[:, b * BLOCK : (b + 1) * BLOCK]
        return total, dot_nn(xg, w_v[cols, :])

    fwd_via = jnp.where(jnp.logical_and(jnp.logical_not(even), has_next), 2 * (s + 1), 0)
    bwd_via = jnp.where(jnp.logical_and(even, has_prev), 16 - 2 * s, 0)
    fwd_relays = jnp.where(jnp.logical_not(even), 2 * (s - 1), 0)
    bwd_relays = jnp.where(jnp.logical_and(even, s <= 4), 12 - 2 * s, 0)

    def remote(src, dst, send, recv, to):
        return pltpu.make_async_remote_copy(
            src_ref=src, dst_ref=dst, send_sem=send, recv_sem=recv,
            device_id=(to, d), device_id_type=MESH,
        )

    def fwd_copy(c):
        return remote(fs.at[c], fr.at[c], fs_s, fs_r.at[c], s + 1)

    def fwd_detour(c):
        return remote(fs.at[c], relay.at[c], fs_s, rl_r.at[c], s + 2)

    def fwd_onward(c):
        return remote(relay.at[c], fr.at[c], rl_s.at[c], fs_r.at[c], s - 1)

    def bwd_copy(c):
        return remote(bs.at[c], next_cot.at[:, at(c)], bs_s, bs_r, s - 1)

    def bwd_detour(c):
        return remote(bs.at[c], relay.at[c], bs_s, rl_r.at[c], s - 2)

    def bwd_onward(c):
        return remote(relay.at[c], next_cot.at[:, at(c)], rl_s.at[c], bs_r, s + 1)

    def core_copy(i):
        return pltpu.make_async_remote_copy(
            src_ref=part.at[2 * i + 1 - core], dst_ref=core_in.at[i],
            send_sem=core_s, recv_sem=core_r.at[i],
            device_id=sibling, device_id_type=MESH,
        )

    def forward(first):
        acc[...] = jnp.zeros_like(acc)
        ss[...] = jnp.zeros_like(ss)

        def f1(p, _):
            piece(FIN, p).wait()

            @pl.when(first)
            def _():
                piece(WG, p).wait()
                piece(WI, p).wait()

            @pl.when(jnp.logical_and(first, p == 1))
            def _():
                start_pieces(WO, SB)

            sq, prod = norm_step(fin_v, p)
            ss[...] += sq
            acc[...] += prod
            return 0

        lax.fori_loop(0, PIECES, f1, 0)

        @pl.when(first)
        def _():
            start_pieces(BIN, COT)
            rb_load.start()

        recip = lax.rsqrt(jnp.sum(ss[...], axis=-1, keepdims=True) / D + EPS_NORM)
        gate_pre = acc[:, 0:R] * recip
        inner = acc[:, R : 2 * R] * recip
        mx[...] = (gate_pre * jax.nn.sigmoid(gate_pre) * inner).astype(BF16)

        @pl.when(first)
        def _():
            pl.semaphore_wait(bar, PEERS)

        idf_load.wait()

        def chosen(slot, cols):
            last = jnp.where(slot == 1, sb_v[1, :, cols], sb_v[2, :, cols])
            return jnp.where(slot == 0, sb_v[0, :, cols], last)

        def f2(c, _):
            @pl.when(lax.rem(c, NC // PIECES) == 0)
            def _():
                piece(SB, c // (NC // PIECES)).wait()

                @pl.when(first)
                def _():
                    piece(WO, c // (NC // PIECES)).wait()

            cols = at(c)
            update = dot_nt(mx[...], wo_v[cols, :])
            for h in range(2):
                rows = slice(h * HALF, (h + 1) * HALF)
                stored = chosen(ids_f[0, h], cols).astype(F32)
                diff = fin_v[rows, cols].astype(F32) + update[rows] - stored
                for b in range(CW // BLOCK):
                    lanes = slice(b * BLOCK, (b + 1) * BLOCK)
                    part_diff = diff[:, lanes]
                    top = jnp.max(jnp.abs(part_diff), axis=-1, keepdims=True)
                    scale = (top + EPS_SCALE).astype(BF16).astype(F32)
                    quantized = (part_diff / scale).astype(BF16)
                    product = scale * quantized.astype(F32)
                    fs[c, rows, lanes] = product.astype(BF16)
                    lane_at = pl.ds(pl.multiple_of(c * CW + b * BLOCK, BLOCK), BLOCK)
                    send_rows[rows, lane_at] = (stored[:, lanes] + product).astype(BF16)

            @pl.when(jnp.logical_and(has_next, jnp.logical_and(c >= fwd_via, jnp.logical_or(even, c < HELD))))
            def _():
                fwd_copy(c).start()

            @pl.when(c < fwd_via)
            def _():
                fwd_detour(c).start()

            return 0

        lax.fori_loop(0, NC, f2, 0)

    def backward(first):
        acc2[...] = jnp.zeros_like(acc2)
        ss[...] = jnp.zeros_like(ss)
        gm[...] = jnp.zeros_like(gm)

        def b1(p, _):
            piece(BIN, p).wait()
            piece(COT, p).wait()

            @pl.when(first)
            def _():
                for kind in (WG, WI, WO):
                    piece(kind, p).wait()

            sq, prod = norm_step(bin_v, p)
            mixed_prod = dot_nn(cot_v[:, span(p)], wo_v[span(p), :])
            ss[...] += sq
            acc2[...] += prod
            gm[...] += mixed_prod
            return 0

        lax.fori_loop(0, PIECES, b1, 0)

        @pl.when(first)
        def _():
            start_pieces(FIN, SB)
            rb_load.start()

        recip_b = lax.rsqrt(jnp.sum(ss[...], axis=-1, keepdims=True) / D + EPS_NORM)
        gate_b = acc2[:, 0:R] * recip_b
        inner_b = acc2[:, R : 2 * R] * recip_b
        sig = jax.nn.sigmoid(gate_b)
        swish = gate_b * sig
        grad_mixed = gm[...]
        gg = grad_mixed * inner_b * sig * (1.0 + gate_b * (1.0 - sig)) * recip_b
        gi = grad_mixed * swish * recip_b
        gcat[:, 0:R] = gg.astype(BF16)
        gcat[:, R : 2 * R] = gi.astype(BF16)
        acc2[:, 0:R] = gg
        acc2[:, R : 2 * R] = gi
        gm[...] = swish * inner_b
        dots = jnp.sum(gg * gate_b + gi * inner_b, axis=-1, keepdims=True)
        krow[...] = jnp.broadcast_to(dots * recip_b * (1.0 / D), (TOK, BLOCK))

        @pl.when(first)
        def _():
            pl.semaphore_wait(bar, PEERS)

        def b2(c, _):
            cols = at(c)
            grad_normed = dot_nt(gcat[...], w_v[cols, :])
            x = bin_v[:, cols].astype(F32)
            for b in range(CW // BLOCK):
                lanes = slice(b * BLOCK, (b + 1) * BLOCK)
                lane_at = pl.ds(pl.multiple_of(c * CW + b * BLOCK, BLOCK), BLOCK)
                passed = (
                    cot_v[:, lane_at].astype(F32)
                    + grad_normed[:, lanes] * gain_v[:, lane_at]
                    - x[:, lanes] * krow[...]
                )
                bs[c, :, lanes] = passed.astype(BF16)

            @pl.when(jnp.logical_and(has_prev, jnp.logical_and(c >= bwd_via, jnp.logical_or(jnp.logical_not(even), c < HELD))))
            def _():
                bwd_copy(c).start()

            @pl.when(c < bwd_via)
            def _():
                bwd_detour(c).start()

            @pl.when(jnp.logical_not(has_next))
            def _():
                next_cot[:, cols] = jnp.zeros((TOK, CW), BF16)

            return 0

        lax.fori_loop(0, NC, b2, 0)

        grad_t[0:R, :] = acc2[:, 0:R].T.astype(BF16)
        grad_t[R : 2 * R, :] = acc2[:, R : 2 * R].T.astype(BF16)
        mixed_t[...] = gm[...].T.astype(BF16)

        def b3(j, _):
            cols = at(j)
            part[j, 0 : 2 * R, :] = dot_nn(grad_t[...], bin_v[:, cols]).astype(BF16)
            part[j, 2 * R : 3 * R, :] = dot_nn(mixed_t[...], cot_v[:, cols]).astype(BF16)

            @pl.when(lax.rem(j, 2) != core)
            def _():
                core_copy(j // 2).start()

            return 0

        lax.fori_loop(0, NC, b3, 0)

    def half(turn, _):
        @pl.when(lax.rem(s + turn, 2) == 0)
        def _():
            forward(turn == 0)

        @pl.when(lax.rem(s + turn, 2) == 1)
        def _():
            backward(turn == 0)

        return 0

    lax.fori_loop(0, 2, half, 0)

    def z_copy(step, h, i):
        return pltpu.make_async_remote_copy(
            src_ref=chip.at[i], dst_ref=z_in.at[step - 1, h],
            send_sem=z_s, recv_sem=z_r.at[step - 1, h],
            device_id=z_peer(step), device_id_type=MESH,
        )

    def chip_sum(k, _):
        h = jnp.where(k < 4, 1 - xh, xh)
        step = lax.rem(k + 1, 4)
        i = lax.rem(z + step, 4) * 2 + h
        core_copy(i).wait_recv()

        def rows_sum(t, _):
            rows = pl.ds(pl.multiple_of(t * 64, 64), 64)
            chip[i, rows, :] = (
                part[2 * i + core, rows, :].astype(F32) + core_in[i, rows, :].astype(F32)
            ).astype(BF16)
            return 0

        lax.fori_loop(0, 6, rows_sum, 0)

        @pl.when(step > 0)
        def _():
            z_copy(step, h, i).start()

        return 0

    lax.fori_loop(0, 8, chip_sum, 0)

    def hand_on(c, _):
        @pl.when(even)
        def _():
            bwd_detour(c).wait_recv()
            bwd_onward(c).start()

        @pl.when(jnp.logical_not(even))
        def _():
            fwd_detour(c).wait_recv()
            fwd_onward(c).start()

        return 0

    relays = fwd_relays + bwd_relays
    lax.fori_loop(0, relays - 4, hand_on, 0)

    x_copy = pltpu.make_async_remote_copy(
        src_ref=x_out, dst_ref=x_in, send_sem=x_sem.at[0], recv_sem=x_sem.at[1],
        device_id=across, device_id_type=MESH,
    )

    def z_sum(h, rows):
        total = chip[2 * z + h, rows, :].astype(F32)
        for step in range(3):
            total += z_in[step, h, rows, :].astype(F32)
        return total

    for step in (1, 2, 3):
        z_copy(step, 1 - xh, 0).wait_recv()

    def other_sum(t, _):
        rows = pl.ds(pl.multiple_of(t * 64, 64), 64)
        x_out[rows, :] = z_sum(1 - xh, rows).astype(BF16)
        return 0

    lax.fori_loop(0, 6, other_sum, 0)
    x_copy.start()

    def send_held(c, _):
        @pl.when(jnp.logical_and(even, has_prev))
        def _():
            bwd_copy(c).start()

        @pl.when(jnp.logical_and(jnp.logical_not(even), has_next))
        def _():
            fwd_copy(c).start()

        return 0

    lax.fori_loop(HELD, NC, send_held, 0)
    lax.fori_loop(jnp.maximum(relays - 4, 0), relays, hand_on, 0)

    fwd_late = jnp.where(even, 2 * s, 0)
    rb_load.wait()
    idr_load.wait()

    def receive(k, _):
        c = lax.rem(k + fwd_late, NC)

        @pl.when(has_prev)
        def _():
            fwd_copy(c).wait_recv()

        @pl.when(jnp.logical_not(has_prev))
        def _():
            fr[c] = jnp.zeros((TOK, CW), BF16)

        cols = at(c)
        for h in range(2):
            rows = slice(h * HALF, (h + 1) * HALF)
            arrived = rb_v[ids_r[0, h], :, cols].astype(F32)
            next_input[rows, cols] = (arrived + fr[c, rows, :].astype(F32)).astype(BF16)
        return 0

    lax.fori_loop(0, LATE, receive, 0)

    for step in (1, 2, 3):
        z_copy(step, xh, 0).wait_recv()
    x_copy.wait_recv()

    def final(t, _):
        lanes = pl.ds(pl.multiple_of(t * BLOCK, BLOCK), BLOCK)
        mine = pl.ds(pl.multiple_of(d * CW + t * BLOCK, BLOCK), BLOCK)
        gain_row = gain_v[:, mine]
        weighted = jnp.zeros((BLOCK, R), F32)
        for a in range(3):
            rows = slice(a * R, (a + 1) * R)
            total = chip[2 * z + xh, rows, lanes].astype(F32)
            for step in range(3):
                total += z_in[step, xh, rows, lanes].astype(F32)
            total += x_in[rows, lanes].astype(F32)
            if a < 2:
                w_rows = w_v[mine, a * R : (a + 1) * R].astype(F32)
                weighted += w_rows * total.T
                total = total * gain_row
            wgrad[lanes, a * R : (a + 1) * R] = total.T
        ggrad[:, lanes] = jnp.sum(weighted.T, axis=0, keepdims=True)
        return 0

    lax.fori_loop(0, CW // BLOCK, final, 0)
    lax.fori_loop(LATE, NC, receive, 0)

    x_copy.wait_send()

    def ended(src, send):
        pltpu.make_async_copy(src, src, send).wait()

    ended(part.at[pl.ds(0, 8)], core_s)
    ended(part.at[pl.ds(0, 6)], z_s)

    def drain_relay(c, _):
        bwd_onward(c).wait_send()
        return 0

    @pl.when(has_next)
    def _():
        ended(fs, fs_s)

    lax.fori_loop(0, relays, drain_relay, 0)

    @pl.when(has_prev)
    def _():
        ended(bs, bs_s)

    @pl.when(has_next)
    def _():
        ended(next_cot, bs_r)


def store(*refs):
    copies = [pltpu.make_async_copy(refs[k], refs[5 + k], refs[10].at[k]) for k in range(5)]
    for c in copies:
        c.start()
    for c in copies:
        c.wait()


def local(
    fwd_input, bwd_input, cotangent, send_buffer, recv_buffer,
    fwd_ids, recv_ids, norm_gain, w_gate, w_in, w_out,
):
    any_spec = pl.BlockSpec(memory_space=pl.ANY)
    dma = pltpu.SemaphoreType.DMA
    wide = (TOK, D)
    chunks = (NC, TOK, CW)
    block = (3 * R, CW)
    outs = pl.pallas_call(
        kernel,
        out_shape=[
            pltpu.VMEM(wide, BF16),
            pltpu.VMEM(wide, BF16),
            pltpu.VMEM(wide, BF16),
            pltpu.VMEM((CW, 3 * R), F32),
            pltpu.VMEM((1, CW), F32),
        ],
        in_specs=[any_spec] * 11,
        out_specs=[pl.BlockSpec(memory_space=pltpu.VMEM)] * 5,
        scratch_shapes=[
            pltpu.VMEM(wide, BF16),
            pltpu.VMEM(wide, BF16),
            pltpu.VMEM(wide, BF16),
            pltpu.VMEM((3, HALF, D), BF16),
            pltpu.VMEM((3, HALF, D), BF16),
            pltpu.VMEM((1, D), F32),
            pltpu.VMEM((D, 2 * R), BF16),
            pltpu.VMEM((D, R), BF16),
            pltpu.VMEM((TOK, 2 * R), F32),
            pltpu.VMEM((TOK, 2 * R), F32),
            pltpu.VMEM((TOK, BLOCK), F32),
            pltpu.VMEM((TOK, R), F32),
            pltpu.VMEM((TOK, R), BF16),
            pltpu.VMEM((TOK, 2 * R), BF16),
            pltpu.VMEM((2 * R, TOK), BF16),
            pltpu.VMEM((R, TOK), BF16),
            pltpu.VMEM((TOK, BLOCK), F32),
            pltpu.VMEM(chunks, BF16),
            pltpu.VMEM(chunks, BF16),
            pltpu.VMEM(chunks, BF16),
            pltpu.VMEM((RELAYS, TOK, CW), BF16),
            pltpu.VMEM((NC,) + block, BF16),
            pltpu.VMEM((8,) + block, BF16),
            pltpu.VMEM((8,) + block, BF16),
            pltpu.VMEM((3, 2) + block, BF16),
            pltpu.VMEM(block, BF16),
            pltpu.VMEM(block, BF16),
            pltpu.SMEM((1, 2), jnp.int32),
            pltpu.SMEM((1, 2), jnp.int32),
            dma((7, PIECES)),
            dma((4,)),
            dma,
            dma((NC,)),
            dma,
            dma,
            dma((RELAYS,)),
            dma((RELAYS,)),
            dma,
            dma((8,)),
            dma,
            dma((3, 2)),
            dma((2,)),
        ],
        compiler_params=pltpu.CompilerParams(
            collective_id=0, has_side_effects=True, vmem_limit_bytes=53 << 20
        ),
        cost_estimate=pl.CostEstimate(
            flops=2 * 11 * TOK * D * R, bytes_accessed=28 << 20, transcendentals=4 * TOK * R
        ),
    )(
        fwd_ids, recv_ids, fwd_input[0], bwd_input[0], cotangent[0], send_buffer[0],
        recv_buffer[0], norm_gain, w_gate[0], w_in[0], w_out[0],
    )
    outs = pl.pallas_call(
        store,
        out_shape=[jax.ShapeDtypeStruct(o.shape, o.dtype) for o in outs],
        in_specs=[pl.BlockSpec(memory_space=pltpu.VMEM)] * 5,
        out_specs=[any_spec] * 5,
        scratch_shapes=[dma((5,))],
        compiler_params=pltpu.CompilerParams(vmem_limit_bytes=2 ** 20),
        cost_estimate=pl.CostEstimate(flops=0, bytes_accessed=7 << 20, transcendentals=0),
    )(*outs)
    return (outs[0][None], outs[1][None], outs[2][None], outs[3][None], outs[4])


def solution(mesh):
    return jax.shard_map(
        local,
        mesh=mesh,
        in_specs=(
            P("section", "dp", None),
            P("section", "dp", None),
            P("section", "dp", None),
            P("section", "dp", None, None),
            P("section", "dp", None, None),
            P("section", "dp"),
            P("section", "dp"),
            P("section", None),
            P("section", None, None),
            P("section", None, None),
            P("section", None, None),
        ),
        out_specs=(
            P("section", "dp", None),
            P("section", "dp", None),
            P("section", "dp", None),
            P("section", "dp", None),
            P("section", "dp"),
        ),
        check_vma=False,
    )
```
